512 devices in a mesh: seq: 32 (over z, core), head: 16 (over x, y).
Axes of the slice: x: 4, y: 4, z: 16, core: 2. Of those that a mesh axis runs over, the one named last changes fastest.
Arguments:
- tokens: bfloat16 [16384, 4096], P('seq', 'head'), may hold values from -8 to 8
- norm_gain: bfloat16 [1, 4096], P(None, 'head'), may hold values from 0.099609375 to 1.8984375
- qkv_weight: bfloat16 [4096, 16, 384], P(None, 'head'), may hold values from -0.109375 to 0.109375
- out_weight: bfloat16 [2048, 4096], P(None, 'head'), may hold values from -0.25 to 0.25
- mem_gate: float32 [16], P('head'), may hold values from -3 to 3
Outputs:
- mixed: bfloat16 [16384, 4096], P('seq', 'head')
The draws below stay inside these ranges and needn't reach their ends.
All inputs are finite; a program needn't handle non-finite values.
Results may differ from the reference program's by a relative error of at most 0.0074.
Values may be sent and summed in bfloat16 or wider, within the bound.
A program may use at most 64 MiB of HBM per device.

```python
import jax
import jax.numpy as jnp
from jax import lax

D = 4096
HD = 128
HEADS = 16
SEG = 2048
TOK_DEV = 512
TOKENS = 16384


def pattern_tables(key):
    key = jax.random.fold_in(key, 103)
    first, second, third, fourth = jax.random.split(key, 4)
    groups = max(HD // 8, 2)
    magnitude = jax.random.uniform(first, (D,), jnp.float32, 0.6, 1.0)
    sign_flip = jnp.where(jax.random.bernoulli(second, 0.5, (D,)), 1.0, -1.0).astype(jnp.float32)
    feature_group = jnp.arange(D, dtype=jnp.int32) % groups
    channel_group = jax.random.permutation(third, HD).astype(jnp.int32) % groups
    value_signs = jnp.where(jax.random.bernoulli(fourth, 0.5, (groups, HD)), 1.0, -1.0).astype(jnp.float32)
    return (groups, magnitude * sign_flip, feature_group, channel_group, value_signs)


def draw_tokens(key, part):
    groups, feature_scale, feature_group, channel_group, value_signs = pattern_tables(key)
    key = jax.random.fold_in(key, 7)
    first = jax.random.fold_in(key, 0)
    second = jax.random.fold_in(key, 1)
    sixth = jax.random.fold_in(key, 5)
    blocks = TOKENS // TOK_DEV
    offsets = jax.random.normal(second, (blocks, D), jnp.float32)
    rise = 1.0 + 2.0 * jnp.arange(blocks, dtype=jnp.float32) / max(blocks - 1, 1)
    moved = jnp.repeat(offsets * rise[:, None] * 0.5, TOK_DEV, axis=0)
    topic = jax.random.randint(sixth, (TOKENS,), 0, groups)
    strength = 1.5 * groups ** 0.5
    pattern = jnp.where(feature_group[None, :] == topic[:, None], strength * feature_scale[None, :], 0.0)
    values = jax.random.normal(first, (TOKENS, D), jnp.float32) + moved + pattern
    return jnp.clip(values, -8.0, 8.0).astype(jnp.bfloat16)


def draw_qkv_weight(key, part):
    groups, feature_scale, feature_group, channel_group, value_signs = pattern_tables(key)
    key = jax.random.fold_in(key, 11)
    first = jax.random.fold_in(key, 0)
    spread = D ** (-0.5)
    values = jnp.clip(jax.random.normal(first, (D, HEADS, 3 * HD), jnp.float32), -6.0, 6.0) * spread
    above = 3.0
    below = 2.0
    inside = channel_group[None, :] == jnp.arange(groups, dtype=jnp.int32)[:, None]
    query_part = jnp.where(inside, above, -below).astype(jnp.float32)
    table = jnp.concatenate([query_part, query_part, value_signs], axis=1)
    reach = 2.0 * groups ** 0.5 / D
    row_terms = table[feature_group] * (feature_scale * reach)[:, None]
    values = values + row_terms[:, None, :]
    return jnp.clip(values, -7.0 * spread, 7.0 * spread).astype(jnp.bfloat16)


def block_levels(rng, extent, cuts, least, high):
    def one(axis_at, blocks):
        steps = jax.random.uniform(jax.random.fold_in(jax.random.fold_in(rng, 6), axis_at), (blocks,), jnp.float32, least / len(cuts), high / len(cuts))
        return jnp.repeat(jnp.exp(steps), extent[axis_at] // blocks).reshape((-1,) + (1,) * (len(extent) - axis_at - 1))

    loudness = one(*cuts[0])
    for cut in cuts[1:]:
        loudness = loudness * one(*cut)
    return loudness


def normal_values(key, shape, width, bound, cuts=(), kind=jnp.bfloat16):
    entries = width * jax.random.normal(key, shape, jnp.float32)
    if cuts:
        entries = entries * block_levels(key, shape, cuts, -0.22, 0.18)
    return jnp.clip(entries, -bound, bound).astype(kind)


def setup_inputs(seed: int = 0) -> dict:
    splits = jax.random.split(jax.random.key(seed), 6)
    return {
        "tokens": draw_tokens(jax.random.fold_in(splits[5], 71), 0),
        "norm_gain": jnp.clip(1.0 + 0.18 * jax.random.normal(splits[1], (1, D), jnp.float32), 0.099609375, 1.8984375).astype(jnp.bfloat16),
        "qkv_weight": draw_qkv_weight(jax.random.fold_in(splits[5], 71), 0),
        "out_weight": normal_values(splits[3], (HEADS * HD, D), (HEADS * HD // 4) ** -0.5, 0.25, ((1, 16),)),
        "mem_gate": jnp.clip(jax.random.uniform(splits[4], (HEADS,), jnp.float32, -3.0, 3.0) * block_levels(splits[4], (HEADS,), ((0, 16),), -0.4, 0.0), -3.0, 3.0),
    }


EPS = 1e-06

def feat(u):
    return jax.nn.elu(u) + 1.0

def reference(tokens, norm_gain, qkv_weight, out_weight, mem_gate):
    xf = tokens.astype(jnp.float32)
    rscale = lax.rsqrt(lax.optimization_barrier(jnp.sum(xf * xf, axis=1)) / D + EPS)
    scaled = (xf * norm_gain.astype(jnp.float32)).astype(jnp.bfloat16)
    nseg = TOKENS // SEG
    causal = jnp.arange(SEG)[:, None] >= jnp.arange(SEG)[None, :]

    def one_head(index):
        weights = lax.dynamic_index_in_dim(qkv_weight, index, 1, keepdims=False)
        raw = jnp.dot(scaled, weights, preferred_element_type=jnp.float32) * rscale[:, None]
        query = raw[:, :HD].astype(jnp.bfloat16).reshape(nseg, SEG, HD)
        keys = raw[:, HD:2 * HD].astype(jnp.bfloat16).reshape(nseg, SEG, HD)
        values = raw[:, 2 * HD:].astype(jnp.bfloat16).reshape(nseg, SEG, HD)
        qf = query.astype(jnp.float32)
        kf = keys.astype(jnp.float32)
        vf = values.astype(jnp.float32)
        scores = jnp.einsum('sqd,skd->sqk', qf, kf) / jnp.sqrt(jnp.float32(HD))
        scores = jnp.where(causal[None], scores, -1e+30)
        top = lax.optimization_barrier(jnp.max(scores, axis=2, keepdims=True))
        expo = jnp.where(causal[None], jnp.exp(scores - top), 0.0)
        probs = (expo / lax.optimization_barrier(jnp.sum(expo, axis=2, keepdims=True))).astype(jnp.bfloat16)
        local = jnp.einsum('sqk,skd->sqd', probs.astype(jnp.float32), vf)
        fk = feat(kf)
        terms = jnp.einsum('ski,skj->sij', fk, vf, precision=lax.Precision.HIGHEST)
        zterms = lax.optimization_barrier(jnp.sum(fk, axis=1))
        memory = jnp.concatenate([jnp.zeros((1, HD, HD), jnp.float32), jnp.cumsum(terms, axis=0)[:-1]], axis=0)
        norm = jnp.concatenate([jnp.zeros((1, HD), jnp.float32), jnp.cumsum(zterms, axis=0)[:-1]], axis=0)
        fq = feat(qf)
        numer = jnp.einsum('sqi,sij->sqj', fq, memory, precision=lax.Precision.HIGHEST)
        denom = jnp.maximum(lax.optimization_barrier(jnp.sum(fq * norm[:, None, :], axis=2)), 1.0)
        retrieved = numer / denom[:, :, None]
        gate = jax.nn.sigmoid(mem_gate[index])
        combined = (gate * retrieved + (1.0 - gate) * local).astype(jnp.bfloat16)
        return combined.reshape(TOKENS, HD)
    combs = lax.map(one_head, jnp.arange(HEADS, dtype=jnp.int32))
    joined = jnp.transpose(combs, (1, 0, 2)).reshape(TOKENS, HEADS * HD)
    return jnp.dot(joined, out_weight, preferred_element_type=jnp.float32).astype(jnp.bfloat16)
```

```python
import functools

import jax
import jax.numpy as jnp
from jax import lax
from jax.experimental import pallas as pl
from jax.experimental.pallas import tpu as pltpu
from jax.sharding import PartitionSpec as P

SEG = 2048
EPS = 1e-06
SIDE = 4
HEADS = SIDE * SIDE
HD = 128
OFFSETS = (0, -1, 1, 2)
MESH = pl.DeviceIdType.MESH
HIGH = lax.Precision.HIGHEST
F32, BF16 = jnp.float32, jnp.bfloat16


def place():
    s, h = lax.axis_index("seq"), lax.axis_index("head")
    return s, h // SIDE, h % SIDE


def around(position, step):
    return lax.rem(position + step + SIDE, SIDE)


def beside(dim, step):
    s, x, y = place()
    if dim == "x":
        return s, around(x, step) * SIDE + y
    return s, x * SIDE + around(y, step)


def greet(partners):
    barrier = pltpu.get_barrier_semaphore()
    for partner in partners:
        pl.semaphore_signal(barrier, inc=1, device_id=partner, device_id_type=MESH)
    pl.semaphore_wait(barrier, len(partners))


def neighbours():
    return [beside(dim, step) for dim in "xy" for step in (1, -1)]


def remote(source, target, sent, landed, partner):
    return pltpu.make_async_remote_copy(
        src_ref=source, dst_ref=target, send_sem=sent, recv_sem=landed,
        device_id=partner, device_id_type=MESH,
    )


class Gather:
    def __init__(self, buf, sent, landed, unit, first_row, rows, dims):
        self.buf, self.sent, self.landed, self.unit = buf, sent, landed, unit
        self.lo, self.rows, self.dims = first_row, rows, dims
        self.started = []

    def slot(self, i, j):
        _, x, y = place()
        along = {self.dims[0]: i, self.dims[1]: j}
        return around(x, along["x"]) * SIDE + around(y, along["y"])

    def view(self, i, j, part):
        half = self.rows // 2
        lo, size = {"all": (0, self.rows), "low": (0, half), "high": (half, half)}[part]
        return self.buf.at[self.slot(i, j), pl.ds(self.lo + lo, size)]

    def copy(self, i, j, part, index, dim, step):
        ref = self.view(i, j, part)
        return remote(ref, ref, self.sent.at[self.unit, index], self.landed.at[self.unit, index], beside(dim, step))

    def send(self, i, j, part, index, dim, step):
        copy = self.copy(i, j, part, index, dim, step)
        copy.start()
        self.started.append(copy)

    def await_first(self, index):
        i, part = ((-1, "all"), (1, "all"), (2, "low"), (2, "high"))[index]
        self.copy(i, 0, part, index, self.dims[0], 1).wait_recv()

    def await_second(self, k, index):
        j, part = ((-1, "all"), (1, "all"), (2, "low"), (2, "high"))[index]
        self.copy(OFFSETS[k], j, part, 4 + 4 * k + index, self.dims[1], 1).wait_recv()

    def out_first(self):
        self.send(0, 0, "all", 0, self.dims[0], 1)
        self.send(0, 0, "all", 1, self.dims[0], -1)

    def out_second(self, k):
        self.send(OFFSETS[k], 0, "all", 4 + 4 * k, self.dims[1], 1)
        self.send(OFFSETS[k], 0, "all", 5 + 4 * k, self.dims[1], -1)

    def on_first(self):
        self.await_first(0)
        self.send(-1, 0, "low", 2, self.dims[0], 1)
        self.out_second(1)
        self.await_first(1)
        self.send(1, 0, "high", 3, self.dims[0], -1)
        self.out_second(2)

    def far_first(self):
        self.await_first(2)
        self.await_first(3)
        self.out_second(3)

    def on_second(self, k):
        self.await_second(k, 0)
        self.send(OFFSETS[k], -1, "low", 6 + 4 * k, self.dims[1], 1)
        self.await_second(k, 1)
        self.send(OFFSETS[k], 1, "high", 7 + 4 * k, self.dims[1], -1)

    def far_second(self, k):
        self.await_second(k, 2)
        self.await_second(k, 3)

    def finish(self):
        for copy in self.started:
            copy.wait_send()


def near_blocks():
    return [(i, j) for i in OFFSETS for j in (0, -1, 1)]


def gather_units(units, multiply):
    pairs = [units[at : at + 2] for at in range(0, len(units), 2)]

    def opening(pair):
        for unit in pair:
            unit.out_first()
        for unit in pair:
            unit.out_second(0)

    def first(pair):
        for unit in pair:
            unit.on_first()

    def second(pair):
        for unit in pair:
            unit.on_second(0)

    def third(pair):
        for unit in pair:
            unit.far_first()

    def fourth(pair):
        for unit in pair:
            unit.on_second(1)
            unit.on_second(2)

    def fifth(pair):
        for unit in pair:
            unit.on_second(3)

    def products(pair):
        for unit in pair:
            multiply(unit, near_blocks(), True)

    def last(pair):
        for unit in pair:
            for k in range(SIDE):
                unit.far_second(k)
            multiply(unit, [(i, 2) for i in OFFSETS], False)

    stages = [opening, first, second, third, fourth, fifth, products, last]
    lag = 2
    for clock in range(len(stages) + lag * (len(pairs) - 1)):
        for at, pair in enumerate(pairs):
            stage = clock - lag * at if clock > 0 else (0 if at < 2 else -1)
            if clock > 0 and at == 1 and stage == 0:
                continue
            if 0 <= stage < len(stages):
                stages[stage](pair)


def make_units(buf, sent, landed, rows, count):
    size = rows // count
    return [
        Gather(buf, sent, landed, u, u * size, size, "yx" if u % 2 == 0 else "xy") for u in range(count)
    ]


def summed_over_plane(own, column, line, sent, landed):
    steps = (1, -1, 2)
    total = own[...]
    copies = []
    for turn, (source, box, dim) in enumerate(((own, column, "y"), (line.at[3], line, "x"))):
        if turn == 1:
            line[3] = total
        turn_copies = []
        for at, step in enumerate(steps):
            index = 3 * turn + at
            copy = remote(source, box.at[at], sent.at[index], landed.at[index], beside(dim, step))
            copy.start()
            turn_copies.append(copy)
        for copy in turn_copies:
            copy.wait_recv()
        for at in range(3):
            total = total + box[at]
        copies += turn_copies
    return total, copies


def qkv_kernel(count, tokens_ref, gain_ref, w_hbm, q_ref, k_ref, v_ref, buf, w_ref, acc, own, column, line,
               sent, landed, small_sent, small_landed, w_sem):
    s, x, y = place()
    w_copy = pltpu.make_async_copy(w_hbm, w_ref, w_sem)
    w_copy.start()
    greet(neighbours() + [beside("x", 2), beside("y", 2)])
    values = tokens_ref[...].astype(F32)
    buf[x * SIDE + y] = (values * gain_ref[...].astype(F32)).astype(BF16)
    rows, width = values.shape
    units = make_units(buf, sent, landed, rows, count)
    waited = []

    def multiply(unit, blocks, first):
        if not waited:
            w_copy.wait()
            waited.append(True)
        at = pl.ds(unit.lo, unit.rows)
        total = None if first else acc[at]
        for i, j in blocks:
            slot = unit.slot(i, j)
            term = jnp.dot(buf[slot, at], w_ref[slot], preferred_element_type=F32)
            total = term if total is None else total + term
        acc[at] = total

    own[...] = lax.dot_general(
        jnp.ones((8, width), F32), values * values, (((1,), (1,)), ((), ())),
        precision=HIGH, preferred_element_type=F32,
    )
    gather_units(units, multiply)
    squares, copies = summed_over_plane(own, column, line, small_sent, small_landed)
    scale = lax.rsqrt(squares / (width * HEADS) + EPS)
    pick = (lax.broadcasted_iota(jnp.int32, (8, HD), 0) == 0).astype(F32)
    spread = lax.dot_general(scale, pick, (((0,), (0,)), ((), ())), precision=HIGH, preferred_element_type=F32)
    q_ref[...] = (acc[:, :HD] * spread).astype(BF16)
    k_ref[...] = (acc[:, HD : 2 * HD] * spread).astype(BF16)
    v_ref[...] = (acc[:, 2 * HD :] * spread).astype(BF16)
    for unit in units:
        unit.finish()
    for copy in copies:
        copy.wait_send()


def project_qkv(tokens, gain, weights):
    rows, width = tokens.shape
    columns = weights.shape[2]
    count = 4
    spec = pl.BlockSpec(memory_space=pltpu.VMEM)
    return pl.pallas_call(
        functools.partial(qkv_kernel, count),
        out_shape=[jax.ShapeDtypeStruct((rows, HD), BF16)] * 3,
        in_specs=[spec, spec, pl.BlockSpec(memory_space=pl.ANY)],
        out_specs=[spec] * 3,
        scratch_shapes=[
            pltpu.VMEM((HEADS, rows, width), BF16),
            pltpu.VMEM((HEADS, width, columns), BF16),
            pltpu.VMEM((rows, columns), F32),
            pltpu.VMEM((8, rows), F32),
            pltpu.VMEM((3, 8, rows), F32),
            pltpu.VMEM((4, 8, rows), F32),
            pltpu.SemaphoreType.DMA((count, 20)),
            pltpu.SemaphoreType.DMA((count, 20)),
            pltpu.SemaphoreType.DMA((6,)),
            pltpu.SemaphoreType.DMA((6,)),
            pltpu.SemaphoreType.DMA,
        ],
        compiler_params=pltpu.CompilerParams(collective_id=0, has_side_effects=True, vmem_limit_bytes=40 << 20),
        name="project_qkv",
    )(tokens, gain, weights)


def out_kernel(count, part_ref, w_hbm, o_ref, buf, w_ref, acc, sent, landed, w_sem):
    s, x, y = place()
    w_copy = pltpu.make_async_copy(w_hbm, w_ref, w_sem)
    w_copy.start()
    greet(neighbours())
    buf[x * SIDE + y] = part_ref[...]
    units = make_units(buf, sent, landed, part_ref.shape[0], count)
    waited = []

    def multiply(unit, blocks, first):
        if not waited:
            w_copy.wait()
            waited.append(True)
        at = pl.ds(unit.lo, unit.rows)
        total = None if first else acc[at]
        for i, j in blocks:
            slot = unit.slot(i, j)
            term = jnp.dot(buf[slot, at], w_ref[slot], preferred_element_type=F32)
            total = term if total is None else total + term
        if first:
            acc[at] = total
        else:
            o_ref[at] = total.astype(BF16)

    gather_units(units, multiply)
    for unit in units:
        unit.finish()


def project_out(part, weights):
    rows = part.shape[0]
    columns = weights.shape[2]
    count = 4
    spec = pl.BlockSpec(memory_space=pltpu.VMEM)
    return pl.pallas_call(
        functools.partial(out_kernel, count),
        out_shape=jax.ShapeDtypeStruct((rows, columns), BF16),
        in_specs=[spec, pl.BlockSpec(memory_space=pl.ANY)],
        out_specs=spec,
        scratch_shapes=[
            pltpu.VMEM((HEADS, rows, HD), BF16),
            pltpu.VMEM((HEADS, HD, columns), BF16),
            pltpu.VMEM((rows, columns), F32),
            pltpu.SemaphoreType.DMA((count, 20)),
            pltpu.SemaphoreType.DMA((count, 20)),
            pltpu.SemaphoreType.DMA,
        ],
        compiler_params=pltpu.CompilerParams(collective_id=1, has_side_effects=True, vmem_limit_bytes=40 << 20),
        name="project_out",
    )(part, weights)


def feat(u):
    return jnp.where(u > 0, u + 1.0, jnp.exp(jnp.minimum(u, 0.0)))


def chip_places():
    s, h = lax.axis_index("seq"), lax.axis_index("head")
    return s, h


SPAN = 4
NORM_ROWS = 16


def attend_kernel(segments, gate_ref, q_ref, k_ref, v_ref, o_ref, kv, o_local, term, parts, seg_term, outgoing, incoming,
                  quarter, memory, kv_sent, kv_landed, a_sent, a_landed, b_sent, b_landed, c_sent, c_landed):
    s, h = chip_places()
    seg, pos = s // SPAN, s % SPAN
    base = seg * SPAN

    def peer(step):
        return base + lax.rem(pos + step, SPAN), h

    mate = (base + lax.rem(pos // 2 * 2 + 1 - pos % 2, SPAN), h)
    across = (base + lax.rem(pos + 2, SPAN), h)
    later = [(lax.rem(s + SPAN * d, segments * SPAN), h) for d in range(1, segments)]
    greet([peer(1), peer(2), peer(3)] + later)

    rows = q_ref.shape[0]
    piece = HD // SPAN
    kv[pos, :, :HD] = k_ref[...]
    kv[pos, :, HD:] = v_ref[...]
    mine = kv.at[pos]
    to_across = remote(mine, mine, kv_sent.at[0], kv_landed.at[0], across)
    to_mate = remote(mine, mine, kv_sent.at[1], kv_landed.at[1], mate)
    to_across.start()
    keys = feat(k_ref[...].astype(F32))
    key_high = keys.astype(BF16)
    term[:HD] = lax.dot_general(key_high, v_ref[...], (((0,), (0,)), ((), ())), preferred_element_type=F32).astype(BF16)
    term[HD:] = jnp.broadcast_to(jnp.sum(keys, axis=0, keepdims=True), (NORM_ROWS, HD)).astype(BF16)
    first = []
    for step in (1, 2, 3):
        to = lax.rem(pos + step, SPAN)
        for at, (lo, size, low) in enumerate(((to * piece, piece, 0), (HD, NORM_ROWS, piece))):
            index = 2 * (step - 1) + at
            copy = remote(term.at[pl.ds(pl.multiple_of(lo, 16), size)], parts.at[step - 1, pl.ds(low, size)],
                          a_sent.at[index], a_landed.at[index], peer(step))
            copy.start()
            first.append(copy)
    to_mate.start()
    for copy in first:
        copy.wait_recv()
    share = jnp.concatenate([term[pl.ds(pl.multiple_of(pos * piece, 16), piece)], term[HD:]], axis=0).astype(F32)
    for at in range(3):
        share = share + parts[at].astype(F32)
    outgoing[...] = share.astype(BF16)

    def second(d):
        return remote(outgoing, incoming.at[d - 1], b_sent.at[d - 1], b_landed.at[d - 1], later[d - 1])

    order = sorted(range(1, segments), key=lambda d: -min(d, segments - d))
    for d in order:
        @pl.when(seg + d < segments)
        def _():
            second(d).start()

    far = lax.rem(pos + 2, SPAN)
    theirs = kv.at[far]
    to_across.wait_recv()
    relay = remote(theirs, theirs, kv_sent.at[2], kv_landed.at[2], mate)
    relay.start()
    to_mate.wait_recv()
    relay.wait_recv()

    factor = float(HD ** -0.5 * 1.4426950408889634)
    chunk = 128
    for r in range(rows // chunk):
        at = pl.ds(r * chunk, chunk)
        query = q_ref[at]
        live_keys = (r + 1) * chunk
        scores = [lax.dot_general(query, kv[pos, :live_keys, :HD], (((1,), (1,)), ((), ())), preferred_element_type=F32)]
        row = lax.broadcasted_iota(jnp.int32, (chunk, live_keys), 0) + r * chunk
        column = lax.broadcasted_iota(jnp.int32, (chunk, live_keys), 1)
        scores[0] = jnp.where(row >= column, scores[0], -1e30)
        tops = [jnp.max(scores[0], axis=1, keepdims=True)]
        biases = [0.0]
        others = []
        for step in (1, 2, 3):
            slot = lax.rem(pos + step, SPAN)
            bias = jnp.where(slot < pos, 0.0, -1e30)
            block = lax.dot_general(query, kv[slot, :, :HD], (((1,), (1,)), ((), ())), preferred_element_type=F32)
            scores.append(block)
            tops.append(jnp.max(block, axis=1, keepdims=True) + bias)
            biases.append(bias)
            others.append(slot)
        top = jnp.maximum(jnp.maximum(tops[0], tops[1]), jnp.maximum(tops[2], tops[3]))
        total = jnp.zeros((chunk, 1), F32)
        mixed = jnp.zeros((chunk, HD), F32)
        for block, bias, value in zip(
            scores, biases, [kv[pos, :live_keys, HD:]] + [kv[slot, :, HD:] for slot in others]
        ):
            expo = jnp.exp2((block - (top - bias)) * factor)
            total = total + jnp.sum(expo, axis=1, keepdims=True)
            mixed = mixed + jnp.dot(expo.astype(BF16), value, preferred_element_type=F32)
        o_local[at] = mixed / total

    share = jnp.zeros((piece + NORM_ROWS, HD), F32)
    quarter[...] = jnp.zeros_like(quarter)
    for d in reversed(order):
        @pl.when(seg - d >= 0)
        def _():
            second(d).wait_recv()
            quarter[...] += incoming[d - 1].astype(F32)
    here = pl.ds(pl.multiple_of(pos * piece, 16), piece)
    memory[here] = quarter[:piece].astype(BF16)
    third = []
    for step in (1, 2, 3):
        copy = remote(memory.at[here], memory.at[here], c_sent.at[step - 1], c_landed.at[step - 1], peer(step))
        copy.start()
        third.append(copy)
    queries = feat(q_ref[...].astype(F32))
    norm = quarter[piece : piece + 1]
    denom = jnp.maximum(jnp.sum(queries * norm, axis=1, keepdims=True), 1.0)
    for step in (1, 2, 3):
        there = pl.ds(pl.multiple_of(lax.rem(pos + SPAN - step, SPAN) * piece, 16), piece)
        remote(memory.at[there], memory.at[there], c_sent.at[step - 1], c_landed.at[step - 1], peer(step)).wait_recv()
    numer = jnp.dot(queries.astype(BF16), memory[...], preferred_element_type=F32)
    gate = jax.nn.sigmoid(jnp.full((1, HD), gate_ref[0], F32))
    o_ref[...] = (gate * (numer / denom) + (1.0 - gate) * o_local[...]).astype(BF16)

    for copy in [to_across, to_mate, relay] + first + third:
        copy.wait_send()
    for d in order:
        @pl.when(seg + d < segments)
        def _():
            second(d).wait_send()


def attend(gate, q, k, v, seq_devices):
    rows = q.shape[0]
    segments = seq_devices // SPAN
    piece = HD // SPAN
    spec = pl.BlockSpec(memory_space=pltpu.VMEM)
    return pl.pallas_call(
        functools.partial(attend_kernel, segments),
        out_shape=jax.ShapeDtypeStruct((rows, HD), BF16),
        in_specs=[pl.BlockSpec(memory_space=pltpu.SMEM), spec, spec, spec],
        out_specs=spec,
        scratch_shapes=[
            pltpu.VMEM((SPAN, rows, 2 * HD), BF16),
            pltpu.VMEM((rows, HD), F32),
            pltpu.VMEM((HD + NORM_ROWS, HD), BF16),
            pltpu.VMEM((3, piece + NORM_ROWS, HD), BF16),
            pltpu.VMEM((piece + NORM_ROWS, HD), F32),
            pltpu.VMEM((piece + NORM_ROWS, HD), BF16),
            pltpu.VMEM((segments - 1, piece + NORM_ROWS, HD), BF16),
            pltpu.VMEM((piece + NORM_ROWS, HD), F32),
            pltpu.VMEM((HD, HD), BF16),
            pltpu.SemaphoreType.DMA((3,)),
            pltpu.SemaphoreType.DMA((3,)),
            pltpu.SemaphoreType.DMA((6,)),
            pltpu.SemaphoreType.DMA((6,)),
            pltpu.SemaphoreType.DMA((segments - 1,)),
            pltpu.SemaphoreType.DMA((segments - 1,)),
            pltpu.SemaphoreType.DMA((3,)),
            pltpu.SemaphoreType.DMA((3,)),
        ],
        compiler_params=pltpu.CompilerParams(collective_id=2, has_side_effects=True, vmem_limit_bytes=40 << 20),
        name="attend",
    )(gate, q, k, v)


def on_device(tokens, norm_gain, qkv_weight, out_weight, mem_gate):
    width = tokens.shape[1]
    weights = qkv_weight.reshape(HEADS, width, 3 * HD)
    q, k, v = project_qkv(tokens, norm_gain, weights)
    part = attend(mem_gate, q, k, v, lax.axis_size("seq"))
    return project_out(part, out_weight.reshape(HEADS, HD, out_weight.shape[1]))


def solution(mesh):
    placed = (P("seq", "head"), P(None, "head"), P(None, "head", None), P(None, "head"), P("head"))
    return jax.shard_map(
        on_device, mesh=mesh, in_specs=placed, out_specs=P("seq", "head"), check_vma=False
    )
```

```python
import functools

import jax
import jax.numpy as jnp
from jax import lax
from jax.experimental import pallas as pl
from jax.experimental.pallas import tpu as pltpu
from jax.sharding import PartitionSpec as P

SEG = 2048
EPS = 1e-06
SIDE = 4
HEADS = SIDE * SIDE
HD = 128
OFFSETS = (0, -1, 1, 2)
MESH = pl.DeviceIdType.MESH
HIGH = lax.Precision.HIGHEST
F32, BF16 = jnp.float32, jnp.bfloat16


def place():
    s, h = lax.axis_index("seq"), lax.axis_index("head")
    return s, h // SIDE, h % SIDE


def around(position, step):
    return lax.rem(position + step + SIDE, SIDE)


def remote(source, target, sent, landed, partner):
    return pltpu.make_async_remote_copy(
        src_ref=source, dst_ref=target, send_sem=sent, recv_sem=landed,
        device_id=partner, device_id_type=MESH,
    )


class Plane:
    def __init__(self):
        s, x, y = place()
        xs = {i: around(x, i) for i in OFFSETS}
        ys = {j: around(y, j) for j in OFFSETS}
        self.slots = {(i, j): xs[i] * SIDE + ys[j] for i in OFFSETS for j in OFFSETS}
        self.devices = {("x", i): (s, self.slots[i, 0]) for i in OFFSETS}
        self.devices.update({("y", j): (s, self.slots[0, j]) for j in OFFSETS})

    def neighbours(self):
        return [self.devices[dim, step] for dim in "xy" for step in (1, -1)]


class Gather:
    def __init__(self, plane, buf, sent, landed, unit, first_row, rows, dims, opposite):
        self.plane, self.buf, self.sent, self.landed, self.unit = plane, buf, sent, landed, unit
        self.at, self.dims, self.opposite = pl.ds(first_row, rows), dims, opposite
        self.started = []

    def slot(self, i, j):
        return self.plane.slots[(i, j) if self.dims == "xy" else (j, i)]

    def copy(self, i, j, index, dim, step):
        ref = self.buf.at[self.slot(i, j), self.at]
        return remote(ref, ref, self.sent.at[self.unit, index], self.landed.at[self.unit, index],
                      self.plane.devices[dim, step])

    def send(self, i, j, index, dim, step):
        copy = self.copy(i, j, index, dim, step)
        copy.start()
        self.started.append(copy)

    def await_first(self, index):
        self.copy((-1, 1, 2)[index], 0, index, self.dims[0], 1).wait_recv()

    def await_second(self, k, index):
        self.copy(OFFSETS[k], (-1, 1, 2)[index], 3 + 3 * k + index, self.dims[1], 1).wait_recv()

    def out_first(self):
        self.send(0, 0, 0, self.dims[0], 1)
        self.send(0, 0, 1, self.dims[0], -1)
        if "first" in self.opposite:
            self.send(0, 0, 2, self.dims[0], 2)

    def out_second(self, k):
        self.send(OFFSETS[k], 0, 3 + 3 * k, self.dims[1], 1)
        self.send(OFFSETS[k], 0, 4 + 3 * k, self.dims[1], -1)
        if k in self.opposite:
            self.send(OFFSETS[k], 0, 5 + 3 * k, self.dims[1], 2)

    def on_first(self):
        way = 1 if self.unit // 2 % 2 == 0 else -1
        order = ((0, -1, 1), (1, 1, 2)) if way == 1 else ((1, 1, 2), (0, -1, 1))
        for turn, (index, i, k) in enumerate(order):
            self.await_first(index)
            if turn == 0 and "first" not in self.opposite:
                self.send(i, 0, 2, self.dims[0], way)
            self.out_second(k)

    def far_first(self):
        self.await_first(2)
        self.out_second(3)

    def on_second(self, k):
        way = 1 if (self.unit // 2 + k) % 2 == 1 else -1
        order = (0, 1) if way == 1 else (1, 0)
        for turn, index in enumerate(order):
            self.await_second(k, index)
            if turn == 0 and k not in self.opposite:
                self.send(OFFSETS[k], -way, 5 + 3 * k, self.dims[1], way)

    def far_second(self, k):
        self.await_second(k, 2)

    def finish(self):
        for copy in self.started:
            copy.wait_send()


def run_units(units, multiply):
    def each(act, *args):
        for unit in units:
            act(unit, *args)

    each(Gather.out_first)
    each(Gather.out_second, 0)
    each(multiply, [(0, 0)])
    each(Gather.on_first)
    each(multiply, [(-1, 0), (1, 0)])
    each(Gather.on_second, 0)
    each(Gather.far_first)
    each(multiply, [(0, -1), (0, 1), (2, 0)])
    for k in (1, 2):
        each(Gather.on_second, k)
    each(multiply, [(i, j) for i in (-1, 1) for j in (-1, 1)])
    each(Gather.on_second, 3)
    each(multiply, [(2, -1), (2, 1)])
    for k in range(SIDE):
        for unit in units:
            unit.far_second(k)
            multiply(unit, [(OFFSETS[k], 2)])


def summed_over_plane(plane, own, column, line, sent, landed):
    steps = (1, -1, 2)
    total = own[...]
    copies = []
    for turn, (source, box, dim) in enumerate(((own, column, "y"), (line.at[3], line, "x"))):
        if turn == 1:
            line[3] = total
        turn_copies = []
        for at, step in enumerate(steps):
            index = 3 * turn + at
            copy = remote(source, box.at[at], sent.at[index], landed.at[index], plane.devices[dim, step])
            copy.start()
            turn_copies.append(copy)
        for copy in turn_copies:
            copy.wait_recv()
        for at in range(3):
            total = total + box[at]
        copies += turn_copies
    return total, copies


def make_units(plane, buf, sent, landed, rows, count, opposite):
    size = rows // count
    return [
        Gather(plane, buf, sent, landed, u, u * size, size, "yx" if u % 2 == 0 else "xy", opposite)
        for u in range(count)
    ]


SPAN = 4
NORM_ROWS = 16
IN_UNITS, OUT_UNITS = 4, 2
FACTOR = float(HD ** -0.5 * 1.4426950408889634)


def feat(u):
    return jnp.where(u > 0, u + 1.0, jnp.exp(jnp.minimum(u, 0.0)))


def product_of(buf, w_ref, acc, finish=None):
    begun, seen = set(), {}

    def multiply(unit, blocks):
        total = acc[unit.at] if unit.unit in begun else None
        for i, j in blocks:
            slot = unit.slot(i, j)
            term = jnp.dot(buf[slot, unit.at], w_ref[slot], preferred_element_type=F32)
            total = term if total is None else total + term
        begun.add(unit.unit)
        seen[unit.unit] = seen.get(unit.unit, 0) + len(blocks)
        if finish is not None and seen[unit.unit] == HEADS:
            finish(unit.at, total)
        else:
            acc[unit.at] = total

    return multiply


def layer_kernel(segments, gate_ref, tokens_hbm, gain_hbm, w_hbm, wo_hbm, o_ref,
                 tokens_ref, gain_ref, w_ref, wo_ref, buf, acc, own, column, line, q_ref, kv, top_ref, sum_ref, local_ref,
                 term, parts, outgoing, incoming, share, memory, obuf, oacc,
                 in_sem, g_sent, g_landed, n_sent, n_landed, kv_sent, kv_landed, a_sent, a_landed, b_sent, b_landed,
                 c_sent, c_landed, o_sent, o_landed):
    loads = [
        pltpu.make_async_copy(source, target, in_sem.at[at])
        for at, (source, target) in enumerate(
            ((tokens_hbm, tokens_ref), (gain_hbm, gain_ref), (w_hbm, w_ref), (wo_hbm, wo_ref))
        )
    ]
    for load in loads:
        load.start()
    plane = Plane()
    s, x, y = place()
    h = x * SIDE + y
    seg, pos = s // SPAN, s % SPAN
    base = seg * SPAN
    peers = {step: (base + lax.rem(pos + step, SPAN), h) for step in (1, 2, 3)}
    mate = (base + pos // 2 * 2 + 1 - pos % 2, h)
    mate_slot = pos // 2 * 2 + 1 - pos % 2
    across, across_slot = peers[2], lax.rem(pos + 2, SPAN)
    relayed_slot = lax.rem(mate_slot + 2, SPAN)
    later = [(lax.rem(s + SPAN * d, segments * SPAN), h) for d in range(1, segments)]
    partners = plane.neighbours() + [plane.devices["x", 2], plane.devices["y", 2]] + list(peers.values()) + later
    barrier = pltpu.get_barrier_semaphore()
    for partner in partners:
        pl.semaphore_signal(barrier, inc=1, device_id=partner, device_id_type=MESH)

    loads[0].wait()
    loads[1].wait()
    values = tokens_ref[...].astype(F32)
    rows, width = values.shape
    buf[h] = (values * gain_ref[...].astype(F32)).astype(BF16)
    own[...] = lax.dot_general(
        jnp.ones((8, width), F32), values * values, (((1,), (1,)), ((), ())),
        precision=HIGH, preferred_element_type=F32,
    )
    pl.semaphore_wait(barrier, len(partners))
    loads[2].wait()
    units = make_units(plane, buf, g_sent, g_landed, rows, IN_UNITS, ())
    run_units(units, product_of(buf, w_ref, acc))

    squares, norm_copies = summed_over_plane(plane, own, column, line, n_sent, n_landed)
    scale = lax.rsqrt(squares / (width * HEADS) + EPS)
    pick = (lax.broadcasted_iota(jnp.int32, (8, HD), 0) == 0).astype(F32)
    spread = lax.dot_general(scale, pick, (((0,), (0,)), ((), ())), precision=HIGH, preferred_element_type=F32)
    keys = (acc[:, HD : 2 * HD] * spread).astype(BF16)
    worth = (acc[:, 2 * HD :] * spread).astype(BF16)
    kv[pos, :, :HD] = keys
    kv[pos, :, HD:] = worth

    mine, theirs = kv.at[pos], kv.at[across_slot]
    to_across = remote(mine, mine, kv_sent.at[0], kv_landed.at[0], across)
    to_mate = remote(mine, mine, kv_sent.at[1], kv_landed.at[1], mate)
    relay = remote(theirs, theirs, kv_sent.at[2], kv_landed.at[2], mate)
    from_across = remote(theirs, theirs, kv_sent.at[0], kv_landed.at[0], across)
    from_mate = remote(kv.at[mate_slot], kv.at[mate_slot], kv_sent.at[1], kv_landed.at[1], mate)
    from_relay = remote(kv.at[relayed_slot], kv.at[relayed_slot], kv_sent.at[2], kv_landed.at[2], mate)

    piece = HD // SPAN
    keys = feat(keys.astype(F32))
    term[:HD] = lax.dot_general(
        keys.astype(BF16), worth, (((0,), (0,)), ((), ())), preferred_element_type=F32
    ).astype(BF16)
    term[HD:] = jnp.broadcast_to(jnp.sum(keys, axis=0, keepdims=True), (NORM_ROWS, HD)).astype(BF16)
    first = []
    for step in (1, 2, 3):
        to = lax.rem(pos + step, SPAN)
        for at, (lo, size, low) in enumerate(((to * piece, piece, 0), (HD, NORM_ROWS, piece))):
            index = 2 * (step - 1) + at
            copy = remote(term.at[pl.ds(pl.multiple_of(lo, 16), size)], parts.at[step - 1, pl.ds(low, size)],
                          a_sent.at[index], a_landed.at[index], peers[step])
            copy.start()
            first.append(copy)
    to_across.start()
    to_mate.start()
    q_ref[...] = (acc[:, :HD] * spread).astype(BF16)
    for copy in first:
        copy.wait_recv()
    here = pl.ds(pl.multiple_of(pos * piece, 16), piece)
    total = jnp.concatenate([term[here], term[HD:]], axis=0).astype(F32)
    for at in range(3):
        total = total + parts[at].astype(F32)
    outgoing[...] = total.astype(BF16)

    def second(d):
        return remote(outgoing, incoming.at[d - 1], b_sent.at[d - 1], b_landed.at[d - 1], later[d - 1])

    order = sorted(range(1, segments), key=lambda d: -min(d, segments - d))
    for d in order:
        @pl.when(seg + d < segments)
        def _():
            second(d).start()

    chunk = 128

    def attend(slot, causal):
        for r in range(rows // chunk):
            at = pl.ds(r * chunk, chunk)
            live = (r + 1) * chunk if causal else rows
            scores = lax.dot_general(
                q_ref[at], kv[slot, :live, :HD], (((1,), (1,)), ((), ())), preferred_element_type=F32
            )
            if causal:
                row = lax.broadcasted_iota(jnp.int32, (chunk, live), 0) + r * chunk
                scores = jnp.where(row >= lax.broadcasted_iota(jnp.int32, (chunk, live), 1), scores, -1e30)
            top = jnp.max(scores, axis=1, keepdims=True)
            if not causal:
                before = top_ref[at]
                top = jnp.maximum(top, before)
                shrink = jnp.exp2((before - top) * FACTOR)
            expo = jnp.exp2((scores - top) * FACTOR)
            weight = jnp.sum(expo, axis=1, keepdims=True)
            mixed = jnp.dot(expo.astype(BF16), kv[slot, :live, HD:], preferred_element_type=F32)
            if not causal:
                weight = weight + sum_ref[at] * shrink
                mixed = mixed + local_ref[at] * shrink
            top_ref[at] = top
            sum_ref[at] = weight
            local_ref[at] = mixed

    attend(pos, True)
    from_mate.wait_recv()

    @pl.when(mate_slot < pos)
    def _():
        attend(mate_slot, False)

    from_across.wait_recv()
    relay.start()

    @pl.when(across_slot < pos)
    def _():
        attend(across_slot, False)

    from_relay.wait_recv()

    @pl.when(relayed_slot < pos)
    def _():
        attend(relayed_slot, False)

    gate = jax.nn.sigmoid(jnp.full((1, HD), gate_ref[0], F32))
    local_ref[...] = local_ref[...] * ((1.0 - gate) / sum_ref[...])
    queries = feat(q_ref[...].astype(F32))

    share[...] = jnp.zeros_like(share)
    for d in reversed(order):
        @pl.when(seg - d >= 0)
        def _():
            second(d).wait_recv()
            share[...] += incoming[d - 1].astype(F32)
    memory[here] = share[:piece].astype(BF16)
    third = []
    for step in (1, 2, 3):
        copy = remote(memory.at[here], memory.at[here], c_sent.at[step - 1], c_landed.at[step - 1], peers[step])
        copy.start()
        third.append(copy)
    denom = jnp.maximum(jnp.sum(queries * share[piece : piece + 1], axis=1, keepdims=True), 1.0)
    for step in (1, 2, 3):
        there = memory.at[pl.ds(pl.multiple_of(lax.rem(pos + SPAN - step, SPAN) * piece, 16), piece)]
        remote(there, there, c_sent.at[step - 1], c_landed.at[step - 1], peers[step]).wait_recv()
    numer = jnp.dot(queries.astype(BF16), memory[...], preferred_element_type=F32)
    obuf[h] = (numer * (gate / denom) + local_ref[...]).astype(BF16)

    loads[3].wait()
    out_units = make_units(plane, obuf, o_sent, o_landed, rows, OUT_UNITS, ("first", 3))

    def finish(at, total):
        o_ref[at] = total.astype(BF16)

    run_units(out_units, product_of(obuf, wo_ref, oacc, finish))

    for unit in units + out_units:
        unit.finish()
    for copy in [to_across, to_mate, relay] + first + third + norm_copies:
        copy.wait_send()
    for d in order:
        @pl.when(seg + d < segments)
        def _():
            second(d).wait_send()


def layer(gate, tokens, gain, weights, out_weights, segments):
    rows, width = tokens.shape
    columns, out_columns = weights.shape[2], out_weights.shape[2]
    piece = HD // SPAN
    anywhere = pl.BlockSpec(memory_space=pl.ANY)
    dma = pltpu.SemaphoreType.DMA
    return pl.pallas_call(
        functools.partial(layer_kernel, segments),
        out_shape=jax.ShapeDtypeStruct((rows, out_columns), BF16),
        in_specs=[pl.BlockSpec(memory_space=pltpu.SMEM)] + [anywhere] * 4,
        out_specs=pl.BlockSpec(memory_space=pltpu.VMEM),
        scratch_shapes=[
            pltpu.VMEM((rows, width), BF16),
            pltpu.VMEM((1, width), BF16),
            pltpu.VMEM((HEADS, width, columns), BF16),
            pltpu.VMEM((HEADS, HD, out_columns), BF16),
            pltpu.VMEM((HEADS, rows, width), BF16),
            pltpu.VMEM((rows, columns), F32),
            pltpu.VMEM((8, rows), F32),
            pltpu.VMEM((3, 8, rows), F32),
            pltpu.VMEM((4, 8, rows), F32),
            pltpu.VMEM((rows, HD), BF16),
            pltpu.VMEM((SPAN, rows, 2 * HD), BF16),
            pltpu.VMEM((rows, 1), F32),
            pltpu.VMEM((rows, 1), F32),
            pltpu.VMEM((rows, HD), F32),
            pltpu.VMEM((HD + NORM_ROWS, HD), BF16),
            pltpu.VMEM((3, piece + NORM_ROWS, HD), BF16),
            pltpu.VMEM((piece + NORM_ROWS, HD), BF16),
            pltpu.VMEM((segments - 1, piece + NORM_ROWS, HD), BF16),
            pltpu.VMEM((piece + NORM_ROWS, HD), F32),
            pltpu.VMEM((HD, HD), BF16),
            pltpu.VMEM((HEADS, rows, HD), BF16),
            pltpu.VMEM((rows, out_columns), F32),
            dma((4,)),
            dma((IN_UNITS, 15)),
            dma((IN_UNITS, 15)),
            dma((6,)),
            dma((6,)),
            dma((3,)),
            dma((3,)),
            dma((6,)),
            dma((6,)),
            dma((segments - 1,)),
            dma((segments - 1,)),
            dma((3,)),
            dma((3,)),
            dma((OUT_UNITS, 15)),
            dma((OUT_UNITS, 15)),
        ],
        compiler_params=pltpu.CompilerParams(collective_id=0, has_side_effects=True, vmem_limit_bytes=56 << 20),
        name="layer",
    )(gate, tokens, gain, weights, out_weights)


def on_device(tokens, norm_gain, qkv_weight, out_weight, mem_gate):
    weights = qkv_weight.reshape(HEADS, tokens.shape[1], 3 * HD)
    out_weights = out_weight.reshape(HEADS, HD, out_weight.shape[1])
    return layer(mem_gate, tokens, norm_gain, weights, out_weights, lax.axis_size("seq") // SPAN)


def solution(mesh):
    placed = (P("seq", "head"), P(None, "head"), P(None, "head", None), P(None, "head"), P("head"))
    return jax.shard_map(
        on_device, mesh=mesh, in_specs=placed, out_specs=P("seq", "head"), check_vma=False
    )
```

```python
import functools

import jax
import jax.numpy as jnp
from jax import lax
from jax.experimental import pallas as pl
from jax.experimental.pallas import tpu as pltpu
from jax.sharding import PartitionSpec as P

SEG = 2048
EPS = 1e-06
SIDE = 4
HEADS = SIDE * SIDE
HD = 128
OFFSETS = (0, -1, 1, 2)
MESH = pl.DeviceIdType.MESH
HIGH = lax.Precision.HIGHEST
F32, BF16 = jnp.float32, jnp.bfloat16


def place():
    s, h = lax.axis_index("seq"), lax.axis_index("head")
    return s, h // SIDE, h % SIDE


def around(position, step):
    return lax.rem(position + step + SIDE, SIDE)


def remote(source, target, sent, landed, partner):
    return pltpu.make_async_remote_copy(
        src_ref=source, dst_ref=target, send_sem=sent, recv_sem=landed,
        device_id=partner, device_id_type=MESH,
    )


class Plane:
    def __init__(self):
        s, x, y = place()
        xs = {i: around(x, i) for i in OFFSETS}
        ys = {j: around(y, j) for j in OFFSETS}
        self.slots = {(i, j): xs[i] * SIDE + ys[j] for i in OFFSETS for j in OFFSETS}
        self.devices = {("x", i): (s, self.slots[i, 0]) for i in OFFSETS}
        self.devices.update({("y", j): (s, self.slots[0, j]) for j in OFFSETS})

    def neighbours(self):
        return [self.devices[dim, step] for dim in "xy" for step in (1, -1)]


class Gather:
    def __init__(self, plane, buf, sent, landed, unit, first_row, rows, dims, opposite):
        self.plane, self.buf, self.sent, self.landed, self.unit = plane, buf, sent, landed, unit
        self.at, self.dims, self.opposite = pl.ds(first_row, rows), dims, opposite
        self.started = []

    def slot(self, i, j):
        return self.plane.slots[(i, j) if self.dims == "xy" else (j, i)]

    def copy(self, i, j, index, dim, step):
        ref = self.buf.at[self.slot(i, j), self.at]
        return remote(ref, ref, self.sent.at[self.unit, index], self.landed.at[self.unit, index],
                      self.plane.devices[dim, step])

    def send(self, i, j, index, dim, step):
        copy = self.copy(i, j, index, dim, step)
        copy.start()
        self.started.append(copy)

    def await_first(self, index):
        self.copy((-1, 1, 2)[index], 0, index, self.dims[0], 1).wait_recv()

    def await_second(self, k, index):
        self.copy(OFFSETS[k], (-1, 1, 2)[index], 3 + 3 * k + index, self.dims[1], 1).wait_recv()

    def out_first(self):
        self.send(0, 0, 0, self.dims[0], 1)
        self.send(0, 0, 1, self.dims[0], -1)
        if "first" in self.opposite:
            self.send(0, 0, 2, self.dims[0], 2)

    def out_second(self, k):
        self.send(OFFSETS[k], 0, 3 + 3 * k, self.dims[1], 1)
        self.send(OFFSETS[k], 0, 4 + 3 * k, self.dims[1], -1)
        if k in self.opposite:
            self.send(OFFSETS[k], 0, 5 + 3 * k, self.dims[1], 2)

    def on_first(self):
        way = 1 if self.unit // 2 % 2 == 0 else -1
        order = ((0, -1, 1), (1, 1, 2)) if way == 1 else ((1, 1, 2), (0, -1, 1))
        for turn, (index, i, k) in enumerate(order):
            self.await_first(index)
            if turn == 0 and "first" not in self.opposite:
                self.send(i, 0, 2, self.dims[0], way)
            self.out_second(k)

    def far_first(self):
        self.await_first(2)
        self.out_second(3)

    def on_second(self, k):
        way = 1 if (self.unit // 2 + k) % 2 == 1 else -1
        order = (0, 1) if way == 1 else (1, 0)
        for turn, index in enumerate(order):
            self.await_second(k, index)
            if turn == 0 and k not in self.opposite:
                self.send(OFFSETS[k], -way, 5 + 3 * k, self.dims[1], way)

    def far_second(self, k):
        self.await_second(k, 2)

    def finish(self):
        for copy in self.started:
            copy.wait_send()


def run_units(units, multiply, between=()):
    between = list(between)

    def each(act, *args):
        for unit in units:
            act(unit, *args)

    def aside():
        if between:
            between.pop(0)()

    each(Gather.out_first)
    each(Gather.out_second, 0)
    aside()
    each(multiply, [(0, 0)])
    each(Gather.on_first)
    aside()
    each(multiply, [(-1, 0), (1, 0)])
    each(Gather.on_second, 0)
    each(Gather.far_first)
    aside()
    each(multiply, [(0, -1), (0, 1), (2, 0)])
    for k in (1, 2):
        each(Gather.on_second, k)
    each(multiply, [(i, j) for i in (-1, 1) for j in (-1, 1)])
    each(Gather.on_second, 3)
    each(multiply, [(2, -1), (2, 1)])
    for k in range(SIDE):
        for unit in units:
            unit.far_second(k)
            multiply(unit, [(OFFSETS[k], 2)])


class PlaneSum:
    def __init__(self, plane, own, column, line, sent, landed):
        self.plane, self.boxes, self.sent, self.landed = plane, (column, line), sent, landed
        self.sources, self.copies = (own, line.at[3]), []

    def start(self, turn):
        for at, step in enumerate((1, -1, 2)):
            index = 3 * turn + at
            copy = remote(self.sources[turn], self.boxes[turn].at[at], self.sent.at[index], self.landed.at[index],
                          self.plane.devices["yx"[turn], step])
            copy.start()
            self.copies.append(copy)

    def total(self, turn):
        for copy in self.copies[3 * turn :]:
            copy.wait_recv()
        box = self.boxes[turn]
        return self.sources[turn][...] + box[0] + box[1] + box[2]

    def pass_on(self):
        self.boxes[1][3] = self.total(0)
        self.start(1)

    def finish(self):
        for copy in self.copies:
            copy.wait_send()


def make_units(plane, buf, sent, landed, rows, count, opposite):
    size = rows // count
    return [
        Gather(plane, buf, sent, landed, u, u * size, size, "yx" if u % 2 == 0 else "xy", opposite)
        for u in range(count)
    ]


SPAN = 4
NORM_ROWS = 16
IN_UNITS, OUT_UNITS = 4, 2
FACTOR = float(HD ** -0.5 * 1.4426950408889634)


def feat(u):
    return jnp.where(u > 0, u + 1.0, jnp.exp(jnp.minimum(u, 0.0)))


def product_of(buf, w_ref, acc, finish=None):
    begun, seen = set(), {}

    def multiply(unit, blocks):
        total = acc[unit.at] if unit.unit in begun else None
        for i, j in blocks:
            slot = unit.slot(i, j)
            term = jnp.dot(buf[slot, unit.at], w_ref[slot], preferred_element_type=F32)
            total = term if total is None else total + term
        begun.add(unit.unit)
        seen[unit.unit] = seen.get(unit.unit, 0) + len(blocks)
        if finish is not None and seen[unit.unit] == HEADS:
            finish(unit.at, total)
        else:
            acc[unit.at] = total

    return multiply


def layer_kernel(segments, gate_ref, tokens_hbm, gain_hbm, w_hbm, wo_hbm, o_ref,
                 tokens_ref, gain_ref, w_ref, wo_ref, buf, acc, own, column, line, spread, q_ref, kv, top_ref, sum_ref, local_ref,
                 term, parts, outgoing, incoming, share, memory, obuf, oacc,
                 ready, in_sem, g_sent, g_landed, n_sent, n_landed, kv_sent, kv_landed, a_sent, a_landed, b_sent, b_landed,
                 c_sent, c_landed, o_sent, o_landed):
    loads = [
        pltpu.make_async_copy(source, target, in_sem.at[at])
        for at, (source, target) in enumerate(
            ((tokens_hbm, tokens_ref), (gain_hbm, gain_ref), (w_hbm, w_ref), (wo_hbm, wo_ref))
        )
    ]
    for load in loads:
        load.start()
    plane = Plane()
    s, x, y = place()
    h = x * SIDE + y
    seg, pos = s // SPAN, s % SPAN
    base = seg * SPAN
    peers = {step: (base + lax.rem(pos + step, SPAN), h) for step in (1, 2, 3)}
    mate = (base + pos // 2 * 2 + 1 - pos % 2, h)
    mate_slot = pos // 2 * 2 + 1 - pos % 2
    across, across_slot = peers[2], lax.rem(pos + 2, SPAN)
    relayed_slot = lax.rem(mate_slot + 2, SPAN)
    later = [(lax.rem(s + SPAN * d, segments * SPAN), h) for d in range(1, segments)]
    partners = plane.neighbours() + [plane.devices["x", 2], plane.devices["y", 2]] + list(peers.values()) + [later[0], later[-1]]
    barrier = pltpu.get_barrier_semaphore()
    for partner in partners:
        pl.semaphore_signal(barrier, inc=1, device_id=partner, device_id_type=MESH)

    loads[0].wait()
    loads[1].wait()
    values = tokens_ref[...].astype(F32)
    rows, width = values.shape
    buf[h] = (values * gain_ref[...].astype(F32)).astype(BF16)
    own[...] = lax.dot_general(
        jnp.ones((8, width), F32), values * values, (((1,), (1,)), ((), ())),
        precision=HIGH, preferred_element_type=F32,
    )
    pl.semaphore_wait(barrier, len(partners))
    loads[2].wait()
    squares = PlaneSum(plane, own, column, line, n_sent, n_landed)
    squares.start(0)

    def scales():
        scale = lax.rsqrt(squares.total(1) / (width * HEADS) + EPS)
        pick = (lax.broadcasted_iota(jnp.int32, (8, HD), 0) == 0).astype(F32)
        spread[...] = lax.dot_general(
            scale, pick, (((0,), (0,)), ((), ())), precision=HIGH, preferred_element_type=F32
        )

    piece = HD // SPAN
    whole = []

    def finish_rows(at, total):
        rscale = spread[at]
        key = (total[:, HD : 2 * HD] * rscale).astype(BF16)
        value = (total[:, 2 * HD :] * rscale).astype(BF16)
        kv[pos, at, :HD] = key
        kv[pos, at, HD:] = value
        key = feat(key.astype(F32))
        product = lax.dot_general(key.astype(BF16), value, (((0,), (0,)), ((), ())), preferred_element_type=F32)
        amount = jnp.sum(key, axis=0, keepdims=True)
        whole[:] = [whole[0] + product, whole[1] + amount] if whole else [product, amount]
        q_ref[at] = (total[:, :HD] * rscale).astype(BF16)

    def tell(turn):
        pl.semaphore_signal(ready.at[turn, 0], inc=1, device_id=later[0], device_id_type=MESH)
        pl.semaphore_signal(ready.at[turn, 1], inc=1, device_id=later[-1], device_id_type=MESH)

    def hear(turn):
        pl.semaphore_wait(ready.at[turn, 0], 1)
        pl.semaphore_wait(ready.at[turn, 1], 1)

    tell(0)

    def early():
        squares.pass_on()
        hear(0)
        tell(1)

    def late():
        scales()
        hear(1)
        tell(2)

    units = make_units(plane, buf, g_sent, g_landed, rows, IN_UNITS, ())
    run_units(units, product_of(buf, w_ref, acc, finish_rows), (lambda: None, early, late))

    mine, theirs = kv.at[pos], kv.at[across_slot]
    to_across = remote(mine, mine, kv_sent.at[0], kv_landed.at[0], across)
    to_mate = remote(mine, mine, kv_sent.at[1], kv_landed.at[1], mate)
    relay = remote(theirs, theirs, kv_sent.at[2], kv_landed.at[2], mate)
    from_across = remote(theirs, theirs, kv_sent.at[0], kv_landed.at[0], across)
    from_mate = remote(kv.at[mate_slot], kv.at[mate_slot], kv_sent.at[1], kv_landed.at[1], mate)
    from_relay = remote(kv.at[relayed_slot], kv.at[relayed_slot], kv_sent.at[2], kv_landed.at[2], mate)

    for at in range(SPAN):
        term[at, :piece] = whole[0][at * piece : (at + 1) * piece].astype(BF16)
        term[at, piece:] = jnp.broadcast_to(whole[1], (NORM_ROWS, HD)).astype(BF16)
    first = []
    for step in (2, 1, 3):
        copy = remote(term.at[lax.rem(pos + step, SPAN)], parts.at[step - 1],
                      a_sent.at[step - 1], a_landed.at[step - 1], peers[step])
        copy.start()
        first.append(copy)

    @pl.when(pos < 2)
    def _():
        to_across.start()

    to_mate.start()
    for copy in first:
        copy.wait_recv()
    here = pl.ds(pl.multiple_of(pos * piece, 16), piece)
    total = term[pos].astype(F32)
    for at in range(3):
        total = total + parts[at].astype(F32)
    outgoing[...] = total.astype(BF16)

    def second(d):
        return remote(outgoing, incoming.at[d - 1], b_sent.at[d - 1], b_landed.at[d - 1], later[d - 1])

    hear(2)
    order = sorted(range(1, segments), key=lambda d: -min(d, segments - d))
    for d in order:
        @pl.when(seg + d < segments)
        def _():
            second(d).start()

    chunk = 128

    def attend(slot, causal):
        for r in range(rows // chunk):
            at = pl.ds(r * chunk, chunk)
            live = (r + 1) * chunk if causal else rows
            scores = lax.dot_general(
                q_ref[at], kv[slot, :live, :HD], (((1,), (1,)), ((), ())), preferred_element_type=F32
            )
            if causal:
                row = lax.broadcasted_iota(jnp.int32, (chunk, live), 0) + r * chunk
                scores = jnp.where(row >= lax.broadcasted_iota(jnp.int32, (chunk, live), 1), scores, -1e30)
            top = jnp.max(scores, axis=1, keepdims=True)
            if not causal:
                before = top_ref[at]
                top = jnp.maximum(top, before)
                shrink = jnp.exp2((before - top) * FACTOR)
            expo = jnp.exp2((scores - top) * FACTOR)
            weight = jnp.sum(expo, axis=1, keepdims=True)
            mixed = jnp.dot(expo.astype(BF16), kv[slot, :live, HD:], preferred_element_type=F32)
            if not causal:
                weight = weight + sum_ref[at] * shrink
                mixed = mixed + local_ref[at] * shrink
            top_ref[at] = top
            sum_ref[at] = weight
            local_ref[at] = mixed

    attend(pos, True)
    from_mate.wait_recv()

    @pl.when(mate_slot < pos)
    def _():
        attend(mate_slot, False)

    @pl.when(pos >= 2)
    def _():
        from_across.wait_recv()
        relay.start()
        attend(across_slot, False)
        from_relay.wait_recv()
        attend(relayed_slot, False)

    gate = jax.nn.sigmoid(jnp.full((1, HD), gate_ref[0], F32))
    local_ref[...] = local_ref[...] * ((1.0 - gate) / sum_ref[...])
    queries = feat(q_ref[...].astype(F32))

    share[...] = jnp.zeros_like(share)
    for d in reversed(order):
        @pl.when(seg - d >= 0)
        def _():
            second(d).wait_recv()
            share[...] += incoming[d - 1].astype(F32)
    memory[here] = share[:piece].astype(BF16)
    third = []
    for step in (1, 2, 3):
        copy = remote(memory.at[here], memory.at[here], c_sent.at[step - 1], c_landed.at[step - 1], peers[step])
        copy.start()
        third.append(copy)
    denom = jnp.maximum(jnp.sum(queries * share[piece : piece + 1], axis=1, keepdims=True), 1.0)
    for step in (1, 2, 3):
        there = memory.at[pl.ds(pl.multiple_of(lax.rem(pos + SPAN - step, SPAN) * piece, 16), piece)]
        remote(there, there, c_sent.at[step - 1], c_landed.at[step - 1], peers[step]).wait_recv()
    numer = jnp.dot(queries.astype(BF16), memory[...], preferred_element_type=F32)
    obuf[h] = (numer * (gate / denom) + local_ref[...]).astype(BF16)

    loads[3].wait()
    out_units = make_units(plane, obuf, o_sent, o_landed, rows, OUT_UNITS, ("first", 3))

    def finish(at, total):
        o_ref[at] = total.astype(BF16)

    run_units(out_units, product_of(obuf, wo_ref, oacc, finish))

    for unit in units + out_units:
        unit.finish()
    squares.finish()
    for copy in [to_mate] + first + third:
        copy.wait_send()

    @pl.when(pos < 2)
    def _():
        to_across.wait_send()

    @pl.when(pos >= 2)
    def _():
        relay.wait_send()

    for d in order:
        @pl.when(seg + d < segments)
        def _():
            second(d).wait_send()


def layer(gate, tokens, gain, weights, out_weights, segments):
    rows, width = tokens.shape
    columns, out_columns = weights.shape[2], out_weights.shape[2]
    piece = HD // SPAN
    anywhere = pl.BlockSpec(memory_space=pl.ANY)
    dma = pltpu.SemaphoreType.DMA
    return pl.pallas_call(
        functools.partial(layer_kernel, segments),
        out_shape=jax.ShapeDtypeStruct((rows, out_columns), BF16),
        in_specs=[pl.BlockSpec(memory_space=pltpu.SMEM)] + [anywhere] * 4,
        out_specs=pl.BlockSpec(memory_space=pltpu.VMEM),
        scratch_shapes=[
            pltpu.VMEM((rows, width), BF16),
            pltpu.VMEM((1, width), BF16),
            pltpu.VMEM((HEADS, width, columns), BF16),
            pltpu.VMEM((HEADS, HD, out_columns), BF16),
            pltpu.VMEM((HEADS, rows, width), BF16),
            pltpu.VMEM((rows, columns), F32),
            pltpu.VMEM((8, rows), F32),
            pltpu.VMEM((3, 8, rows), F32),
            pltpu.VMEM((4, 8, rows), F32),
            pltpu.VMEM((rows, HD), F32),
            pltpu.VMEM((rows, HD), BF16),
            pltpu.VMEM((SPAN, rows, 2 * HD), BF16),
            pltpu.VMEM((rows, 1), F32),
            pltpu.VMEM((rows, 1), F32),
            pltpu.VMEM((rows, HD), F32),
            pltpu.VMEM((SPAN, piece + NORM_ROWS, HD), BF16),
            pltpu.VMEM((3, piece + NORM_ROWS, HD), BF16),
            pltpu.VMEM((piece + NORM_ROWS, HD), BF16),
            pltpu.VMEM((segments - 1, piece + NORM_ROWS, HD), BF16),
            pltpu.VMEM((piece + NORM_ROWS, HD), F32),
            pltpu.VMEM((HD, HD), BF16),
            pltpu.VMEM((HEADS, rows, HD), BF16),
            pltpu.VMEM((rows, out_columns), F32),
            pltpu.SemaphoreType.REGULAR((3, 2)),
            dma((4,)),
            dma((IN_UNITS, 15)),
            dma((IN_UNITS, 15)),
            dma((6,)),
            dma((6,)),
            dma((3,)),
            dma((3,)),
            dma((3,)),
            dma((3,)),
            dma((segments - 1,)),
            dma((segments - 1,)),
            dma((3,)),
            dma((3,)),
            dma((OUT_UNITS, 15)),
            dma((OUT_UNITS, 15)),
        ],
        compiler_params=pltpu.CompilerParams(collective_id=0, has_side_effects=True, vmem_limit_bytes=56 << 20),
        name="layer",
    )(gate, tokens, gain, weights, out_weights)


def on_device(tokens, norm_gain, qkv_weight, out_weight, mem_gate):
    weights = qkv_weight.reshape(HEADS, tokens.shape[1], 3 * HD)
    out_weights = out_weight.reshape(HEADS, HD, out_weight.shape[1])
    return layer(mem_gate, tokens, norm_gain, weights, out_weights, lax.axis_size("seq") // SPAN)


def solution(mesh):
    placed = (P("seq", "head"), P(None, "head"), P(None, "head", None), P(None, "head"), P("head"))
    return jax.shard_map(
        on_device, mesh=mesh, in_specs=placed, out_specs=P("seq", "head"), check_vma=False
    )
```

```python
import functools

import jax
import jax.numpy as jnp
from jax import lax
from jax.experimental import pallas as pl
from jax.experimental.pallas import tpu as pltpu
from jax.sharding import PartitionSpec as P

SEG = 2048
EPS = 1e-06
SIDE = 4
HEADS = SIDE * SIDE
HD = 128
OFFSETS = (0, -1, 1, 2)
MESH = pl.DeviceIdType.MESH
HIGH = lax.Precision.HIGHEST
F32, BF16 = jnp.float32, jnp.bfloat16


def place():
    s, h = lax.axis_index("seq"), lax.axis_index("head")
    return s, h // SIDE, h % SIDE


def around(position, step):
    return lax.rem(position + step + SIDE, SIDE)


def remote(source, target, sent, landed, partner):
    return pltpu.make_async_remote_copy(
        src_ref=source, dst_ref=target, send_sem=sent, recv_sem=landed,
        device_id=partner, device_id_type=MESH,
    )


class Plane:
    def __init__(self):
        s, x, y = place()
        xs = {i: around(x, i) for i in OFFSETS}
        ys = {j: around(y, j) for j in OFFSETS}
        self.slots = {(i, j): xs[i] * SIDE + ys[j] for i in OFFSETS for j in OFFSETS}
        self.devices = {("x", i): (s, self.slots[i, 0]) for i in OFFSETS}
        self.devices.update({("y", j): (s, self.slots[0, j]) for j in OFFSETS})

    def neighbours(self):
        return [self.devices[dim, step] for dim in "xy" for step in (1, -1)]


class Gather:
    def __init__(self, plane, buf, sent, landed, unit, first_row, rows, dims, opposite):
        self.plane, self.buf, self.sent, self.landed, self.unit = plane, buf, sent, landed, unit
        self.lo, self.rows, self.dims, self.opposite = first_row, rows, dims, opposite
        self.at = pl.ds(first_row, rows)
        self.started = []

    def slot(self, i, j):
        return self.plane.slots[(i, j) if self.dims == "xy" else (j, i)]

    def copy(self, i, j, index, dim, step):
        ref = self.buf.at[self.slot(i, j), self.at]
        return remote(ref, ref, self.sent.at[self.unit, index], self.landed.at[self.unit, index],
                      self.plane.devices[dim, step])

    def send(self, i, j, index, dim, step):
        copy = self.copy(i, j, index, dim, step)
        copy.start()
        self.started.append(copy)

    def await_first(self, index):
        self.copy((-1, 1, 2)[index], 0, index, self.dims[0], 1).wait_recv()

    def await_second(self, k, index):
        self.copy(OFFSETS[k], (-1, 1, 2)[index], 3 + 3 * k + index, self.dims[1], 1).wait_recv()

    def out_first(self):
        self.send(0, 0, 0, self.dims[0], 1)
        self.send(0, 0, 1, self.dims[0], -1)
        if "first" in self.opposite:
            self.send(0, 0, 2, self.dims[0], 2)

    def out_second(self, k):
        self.send(OFFSETS[k], 0, 3 + 3 * k, self.dims[1], 1)
        self.send(OFFSETS[k], 0, 4 + 3 * k, self.dims[1], -1)
        if k in self.opposite:
            self.send(OFFSETS[k], 0, 5 + 3 * k, self.dims[1], 2)

    def on_first(self):
        way = 1 if self.unit % 2 == 0 else -1
        order = ((0, -1, 1), (1, 1, 2)) if way == 1 else ((1, 1, 2), (0, -1, 1))
        for turn, (index, i, k) in enumerate(order):
            self.await_first(index)
            if turn == 0 and "first" not in self.opposite:
                self.send(i, 0, 2, self.dims[0], way)
            self.out_second(k)

    def far_first(self):
        self.await_first(2)
        self.out_second(3)

    def on_second(self, k):
        way = 1 if (self.unit + k) % 2 == 1 else -1
        order = (0, 1) if way == 1 else (1, 0)
        for turn, index in enumerate(order):
            self.await_second(k, index)
            if turn == 0 and k not in self.opposite:
                self.send(OFFSETS[k], -way, 5 + 3 * k, self.dims[1], way)

    def far_second(self, k):
        self.await_second(k, 2)

    def finish(self):
        for copy in self.started:
            copy.wait_send()


def run_units(units, multiply, between=()):
    between = list(between)
    half = len(units) // 2
    groups = [units[:half], units[half:]]

    def each(act, *args):
        for at in range(half):
            for group in groups:
                act(group[at], *args)

    def product(blocks):
        for group in groups:
            for unit in group:
                multiply([unit], blocks)

    def aside():
        if between:
            between.pop(0)()

    each(Gather.out_first)
    each(Gather.out_second, 0)
    aside()
    product([(0, 0)])
    each(Gather.on_first)
    aside()
    product([(-1, 0), (1, 0)])
    each(Gather.on_second, 0)
    each(Gather.far_first)
    aside()
    product([(0, -1), (0, 1), (2, 0)])
    aside()
    for k in (1, 2):
        each(Gather.on_second, k)
    product([(i, j) for i in (-1, 1) for j in (-1, 1)])
    aside()
    each(Gather.on_second, 3)
    product([(2, -1), (2, 1)])
    aside()
    for k in range(SIDE - 1):
        each(Gather.far_second, k)
        product([(OFFSETS[k], 2)])
        aside()
    for at in range(half):
        for group in groups:
            group[at].far_second(SIDE - 1)
            multiply([group[at]], [(OFFSETS[SIDE - 1], 2)])


class PlaneSum:
    def __init__(self, plane, own, column, line, sent, landed):
        self.plane, self.boxes, self.sent, self.landed = plane, (column, line), sent, landed
        self.sources, self.copies = (own, line.at[3]), []

    def start(self, turn):
        for at, step in enumerate((1, -1, 2)):
            index = 3 * turn + at
            copy = remote(self.sources[turn], self.boxes[turn].at[at], self.sent.at[index], self.landed.at[index],
                          self.plane.devices["yx"[turn], step])
            copy.start()
            self.copies.append(copy)

    def total(self, turn):
        for copy in self.copies[3 * turn :]:
            copy.wait_recv()
        box = self.boxes[turn]
        return self.sources[turn][...] + box[0] + box[1] + box[2]

    def pass_on(self):
        self.boxes[1][3] = self.total(0)
        self.start(1)

    def finish(self):
        for copy in self.copies:
            copy.wait_send()


def make_units(plane, buf, sent, landed, rows, count, opposite):
    size = rows // count
    return [
        Gather(plane, buf, sent, landed, u, u * size, size, "yx" if u < count // 2 else "xy", opposite)
        for u in range(count)
    ]


SPAN = 4
NORM_ROWS = 16
IN_UNITS, OUT_UNITS = 4, 2
FACTOR = float(HD ** -0.5 * 1.4426950408889634)


def feat(u):
    return jnp.where(u > 0, u + 1.0, jnp.exp(jnp.minimum(u, 0.0)))


def product_of(buf, w_ref, acc, finish=None):
    begun, seen = set(), {}

    def multiply(units, blocks):
        at = pl.ds(units[0].lo, sum(unit.rows for unit in units))
        key = tuple(unit.unit for unit in units)
        total = acc[at] if begun.issuperset(key) else None
        for i, j in blocks:
            slot = units[0].slot(i, j)
            term = jnp.dot(buf[slot, at], w_ref[slot], preferred_element_type=F32)
            total = term if total is None else total + term
        begun.update(key)
        for one in key:
            seen[one] = seen.get(one, 0) + len(blocks)
        if finish is not None and seen[key[0]] == HEADS:
            finish(units[0], total)
        else:
            acc[at] = total

    return multiply


def layer_kernel(segments, gate_ref, tokens_hbm, gain_hbm, w_hbm, wo_hbm, o_ref,
                 tokens_ref, gain_ref, w_ref, wo_ref, buf, acc, own, column, line, spread, q_ref, kv, top_ref, sum_ref, local_ref,
                 term, parts, outgoing, incoming, share, memory, obuf, oacc,
                 ready, in_sem, g_sent, g_landed, n_sent, n_landed, kv_sent, kv_landed, a_sent, a_landed, b_sent, b_landed,
                 c_sent, c_landed, o_sent, o_landed):
    loads = [
        pltpu.make_async_copy(source, target, in_sem.at[at])
        for at, (source, target) in enumerate(
            ((tokens_hbm, tokens_ref), (gain_hbm, gain_ref), (w_hbm, w_ref), (wo_hbm, wo_ref))
        )
    ]
    for load in loads:
        load.start()
    plane = Plane()
    s, x, y = place()
    h = x * SIDE + y
    seg, pos = s // SPAN, s % SPAN
    base = seg * SPAN
    peers = {step: (base + lax.rem(pos + step, SPAN), h) for step in (1, 2, 3)}
    mate = (base + pos // 2 * 2 + 1 - pos % 2, h)
    mate_slot = pos // 2 * 2 + 1 - pos % 2
    across, across_slot = peers[2], lax.rem(pos + 2, SPAN)
    relayed_slot = lax.rem(mate_slot + 2, SPAN)
    later = [(lax.rem(s + SPAN * d, segments * SPAN), h) for d in range(1, segments)]
    partners = plane.neighbours() + [plane.devices["x", 2], plane.devices["y", 2]] + list(peers.values())
    barrier = pltpu.get_barrier_semaphore()
    for partner in partners:
        pl.semaphore_signal(barrier, inc=1, device_id=partner, device_id_type=MESH)

    for d in range(1, segments):
        @pl.when(seg + d < segments)
        def _():
            pl.semaphore_signal(barrier, inc=1, device_id=later[d - 1], device_id_type=MESH)

    loads[0].wait()
    loads[1].wait()
    values = tokens_ref[...].astype(F32)
    rows, width = values.shape
    buf[h] = (values * gain_ref[...].astype(F32)).astype(BF16)
    own[...] = lax.dot_general(
        jnp.ones((8, width), F32), values * values, (((1,), (1,)), ((), ())),
        precision=HIGH, preferred_element_type=F32,
    )
    pl.semaphore_wait(barrier, len(partners) + seg)

    squares = PlaneSum(plane, own, column, line, n_sent, n_landed)

    def scales():
        scale = lax.rsqrt(squares.total(1) / (width * HEADS) + EPS)
        pick = (lax.broadcasted_iota(jnp.int32, (8, HD), 0) == 0).astype(F32)
        spread[...] = lax.dot_general(
            scale, pick, (((0,), (0,)), ((), ())), precision=HIGH, preferred_element_type=F32
        )

    piece = HD // SPAN
    whole = []
    size = rows // IN_UNITS

    def over(slot, unit, to):
        ref = kv.at[slot, pl.ds(unit * size, size)]
        return remote(ref, ref, kv_sent.at[1 + unit], kv_landed.at[1 + unit], to)

    def relay(slot, unit):
        ref = kv.at[slot, pl.ds(unit * size, size)]
        at = 1 + IN_UNITS + unit
        return remote(ref, ref, kv_sent.at[at], kv_landed.at[at], mate)


    def finish_rows(unit, total):
        at = unit.at
        rscale = spread[at]
        key = (total[:, HD : 2 * HD] * rscale).astype(BF16)
        value = (total[:, 2 * HD :] * rscale).astype(BF16)
        kv[pos, at, :HD] = key
        kv[pos, at, HD:] = value
        key = feat(key.astype(F32))
        product = lax.dot_general(key.astype(BF16), value, (((0,), (0,)), ((), ())), preferred_element_type=F32)
        amount = jnp.sum(key, axis=0, keepdims=True)
        whole[:] = [whole[0] + product, whole[1] + amount] if whole else [product, amount]
        q_ref[at] = (total[:, :HD] * rscale).astype(BF16)

    def begin():
        squares.start(0)
        loads[2].wait()
        for d in range(1, segments):
            @pl.when(seg - d >= 0)
            def _():
                pl.semaphore_signal(ready.at[d - 1], inc=1, device_id=later[segments - d - 1], device_id_type=MESH)

    units = make_units(plane, buf, g_sent, g_landed, rows, IN_UNITS, ())
    run_units(units, product_of(buf, w_ref, acc, finish_rows), [begin, squares.pass_on, scales])

    to_mate = remote(kv.at[pos], kv.at[pos], kv_sent.at[0], kv_landed.at[0], mate)
    from_mate = remote(kv.at[mate_slot], kv.at[mate_slot], kv_sent.at[0], kv_landed.at[0], mate)

    for at in range(SPAN):
        term[at, :piece] = whole[0][at * piece : (at + 1) * piece].astype(BF16)
        term[at, piece:] = jnp.broadcast_to(whole[1], (NORM_ROWS, HD)).astype(BF16)
    first = []
    for step in (2, 1, 3):
        copy = remote(term.at[lax.rem(pos + step, SPAN)], parts.at[step - 1],
                      a_sent.at[step - 1], a_landed.at[step - 1], peers[step])
        copy.start()
        first.append(copy)

    @pl.when(pos < 2)
    def _():
        for unit in range(IN_UNITS):
            over(pos, unit, across).start()

    to_mate.start()
    for copy in first:
        copy.wait_recv()
    here = pl.ds(pl.multiple_of(pos * piece, 16), piece)
    total = term[pos].astype(F32)
    for at in range(3):
        total = total + parts[at].astype(F32)
    outgoing[...] = total.astype(BF16)

    def second(d):
        return remote(outgoing, incoming.at[d - 1], b_sent.at[d - 1], b_landed.at[d - 1], later[d - 1])

    order = sorted(range(1, segments), key=lambda d: -min(d, segments - d))
    for d in order:
        @pl.when(seg + d < segments)
        def _():
            pl.semaphore_wait(ready.at[d - 1], 1)
            second(d).start()

    chunk = 128

    def attend(slot, causal):
        for r in range(rows // chunk):
            at = pl.ds(r * chunk, chunk)
            live = (r + 1) * chunk if causal else rows
            scores = lax.dot_general(
                q_ref[at], kv[slot, :live, :HD], (((1,), (1,)), ((), ())), preferred_element_type=F32
            )
            if causal:
                row = lax.broadcasted_iota(jnp.int32, (chunk, live), 0) + r * chunk
                scores = jnp.where(row >= lax.broadcasted_iota(jnp.int32, (chunk, live), 1), scores, -1e30)
            top = jnp.max(scores, axis=1, keepdims=True)
            if not causal:
                before = top_ref[at]
                top = jnp.maximum(top, before)
                shrink = jnp.exp2((before - top) * FACTOR)
            expo = jnp.exp2((scores - top) * FACTOR)
            weight = jnp.sum(expo, axis=1, keepdims=True)
            mixed = jnp.dot(expo.astype(BF16), kv[slot, :live, HD:], preferred_element_type=F32)
            if not causal:
                weight = weight + sum_ref[at] * shrink
                mixed = mixed + local_ref[at] * shrink
            top_ref[at] = top
            sum_ref[at] = weight
            local_ref[at] = mixed

    attend(pos, True)
    from_mate.wait_recv()

    @pl.when(mate_slot < pos)
    def _():
        attend(mate_slot, False)

    @pl.when(pos >= 2)
    def _():
        for unit in range(IN_UNITS):
            over(across_slot, unit, across).wait_recv()
            relay(across_slot, unit).start()
        attend(across_slot, False)
        for unit in range(IN_UNITS):
            relay(relayed_slot, unit).wait_recv()
        attend(relayed_slot, False)

    gate = jax.nn.sigmoid(jnp.full((1, HD), gate_ref[0], F32))
    local_ref[...] = local_ref[...] * ((1.0 - gate) / sum_ref[...])
    queries = feat(q_ref[...].astype(F32)).astype(BF16)

    share[...] = jnp.zeros_like(share)
    for d in reversed(order):
        @pl.when(seg - d >= 0)
        def _():
            second(d).wait_recv()
            share[...] += incoming[d - 1].astype(F32)
    memory[here] = share[:piece].astype(BF16)
    third = []
    for step in (1, 2, 3):
        copy = remote(memory.at[here], memory.at[here], c_sent.at[step - 1], c_landed.at[step - 1], peers[step])
        copy.start()
        third.append(copy)
    pick = (lax.broadcasted_iota(jnp.int32, (8, HD), 0) == 0).astype(F32)
    norm = lax.dot_general(
        share[piece : piece + 8], pick, (((0,), (0,)), ((), ())), precision=HIGH, preferred_element_type=F32
    )
    denom = jnp.dot(queries, norm.astype(BF16), preferred_element_type=F32)
    weight = gate / jnp.maximum(denom, 1.0)
    for step in (1, 2, 3):
        there = memory.at[pl.ds(pl.multiple_of(lax.rem(pos + SPAN - step, SPAN) * piece, 16), piece)]
        remote(there, there, c_sent.at[step - 1], c_landed.at[step - 1], peers[step]).wait_recv()
    numer = jnp.dot(queries, memory[...], preferred_element_type=F32)
    obuf[h] = (numer * weight + local_ref[...]).astype(BF16)

    loads[3].wait()
    out_units = make_units(plane, obuf, o_sent, o_landed, rows, OUT_UNITS, ("first",))

    def finish(unit, total):
        o_ref[unit.at] = total.astype(BF16)

    run_units(out_units, product_of(obuf, wo_ref, oacc, finish))

    for unit in units + out_units:
        unit.finish()
    squares.finish()
    for copy in [to_mate] + first + third:
        copy.wait_send()

    @pl.when(pos < 2)
    def _():
        for unit in range(IN_UNITS):
            over(pos, unit, across).wait_send()

    @pl.when(pos >= 2)
    def _():
        for unit in range(IN_UNITS):
            relay(across_slot, unit).wait_send()

    for d in order:
        @pl.when(seg + d < segments)
        def _():
            second(d).wait_send()


def layer(gate, tokens, gain, weights, out_weights, segments):
    rows, width = tokens.shape
    columns, out_columns = weights.shape[2], out_weights.shape[2]
    piece = HD // SPAN
    anywhere = pl.BlockSpec(memory_space=pl.ANY)
    dma = pltpu.SemaphoreType.DMA
    return pl.pallas_call(
        functools.partial(layer_kernel, segments),
        out_shape=jax.ShapeDtypeStruct((rows, out_columns), BF16),
        in_specs=[pl.BlockSpec(memory_space=pltpu.SMEM)] + [anywhere] * 4,
        out_specs=pl.BlockSpec(memory_space=pltpu.VMEM),
        scratch_shapes=[
            pltpu.VMEM((rows, width), BF16),
            pltpu.VMEM((1, width), BF16),
            pltpu.VMEM((HEADS, width, columns), BF16),
            pltpu.VMEM((HEADS, HD, out_columns), BF16),
            pltpu.VMEM((HEADS, rows, width), BF16),
            pltpu.VMEM((rows, columns), F32),
            pltpu.VMEM((8, rows), F32),
            pltpu.VMEM((3, 8, rows), F32),
            pltpu.VMEM((4, 8, rows), F32),
            pltpu.VMEM((rows, HD), F32),
            pltpu.VMEM((rows, HD), BF16),
            pltpu.VMEM((SPAN, rows, 2 * HD), BF16),
            pltpu.VMEM((rows, 1), F32),
            pltpu.VMEM((rows, 1), F32),
            pltpu.VMEM((rows, HD), F32),
            pltpu.VMEM((SPAN, piece + NORM_ROWS, HD), BF16),
            pltpu.VMEM((3, piece + NORM_ROWS, HD), BF16),
            pltpu.VMEM((piece + NORM_ROWS, HD), BF16),
            pltpu.VMEM((segments - 1, piece + NORM_ROWS, HD), BF16),
            pltpu.VMEM((piece + NORM_ROWS, HD), F32),
            pltpu.VMEM((HD, HD), BF16),
            pltpu.VMEM((HEADS, rows, HD), BF16),
            pltpu.VMEM((rows, out_columns), F32),
            pltpu.SemaphoreType.REGULAR((segments - 1,)),
            dma((4,)),
            dma((IN_UNITS, 15)),
            dma((IN_UNITS, 15)),
            dma((6,)),
            dma((6,)),
            dma((1 + 2 * IN_UNITS,)),
            dma((1 + 2 * IN_UNITS,)),
            dma((3,)),
            dma((3,)),
            dma((segments - 1,)),
            dma((segments - 1,)),
            dma((3,)),
            dma((3,)),
            dma((OUT_UNITS, 15)),
            dma((OUT_UNITS, 15)),
        ],
        compiler_params=pltpu.CompilerParams(collective_id=0, has_side_effects=True, vmem_limit_bytes=56 << 20),
        name="layer",
    )(gate, tokens, gain, weights, out_weights)


def on_device(tokens, norm_gain, qkv_weight, out_weight, mem_gate):
    weights = qkv_weight.reshape(HEADS, tokens.shape[1], 3 * HD)
    out_weights = out_weight.reshape(HEADS, HD, out_weight.shape[1])
    return layer(mem_gate, tokens, norm_gain, weights, out_weights, lax.axis_size("seq") // SPAN)


def solution(mesh):
    placed = (P("seq", "head"), P(None, "head"), P(None, "head", None), P(None, "head"), P("head"))
    return jax.shard_map(
        on_device, mesh=mesh, in_specs=placed, out_specs=P("seq", "head"), check_vma=False
    )
```

```python
import functools

import jax
import jax.numpy as jnp
from jax import lax
from jax.experimental import pallas as pl
from jax.experimental.pallas import tpu as pltpu
from jax.sharding import PartitionSpec as P

SEG = 2048
EPS = 1e-06
SIDE = 4
HEADS = SIDE * SIDE
HD = 128
OFFSETS = (0, -1, 1, 2)
MESH = pl.DeviceIdType.MESH
HIGH = lax.Precision.HIGHEST
F32, BF16 = jnp.float32, jnp.bfloat16


def place():
    s, h = lax.axis_index("seq"), lax.axis_index("head")
    return s, h // SIDE, h % SIDE


def around(position, step):
    return lax.rem(position + step + SIDE, SIDE)


def remote(source, target, sent, landed, partner):
    return pltpu.make_async_remote_copy(
        src_ref=source, dst_ref=target, send_sem=sent, recv_sem=landed,
        device_id=partner, device_id_type=MESH,
    )


class Plane:
    def __init__(self):
        s, x, y = place()
        xs = {i: around(x, i) for i in OFFSETS}
        ys = {j: around(y, j) for j in OFFSETS}
        self.slots = {(i, j): xs[i] * SIDE + ys[j] for i in OFFSETS for j in OFFSETS}
        self.devices = {("x", i): (s, self.slots[i, 0]) for i in OFFSETS}
        self.devices.update({("y", j): (s, self.slots[0, j]) for j in OFFSETS})

    def neighbours(self):
        return [self.devices[dim, step] for dim in "xy" for step in (1, -1)]


class Gather:
    def __init__(self, plane, buf, sent, landed, unit, first_row, rows, dims, opposite):
        self.plane, self.buf, self.sent, self.landed, self.unit = plane, buf, sent, landed, unit
        self.lo, self.rows, self.dims, self.opposite = first_row, rows, dims, opposite
        self.at = pl.ds(first_row, rows)
        self.started = []

    def slot(self, i, j):
        return self.plane.slots[(i, j) if self.dims == "xy" else (j, i)]

    def copy(self, i, j, index, dim, step):
        ref = self.buf.at[self.slot(i, j), self.at]
        return remote(ref, ref, self.sent.at[self.unit, index], self.landed.at[self.unit, index],
                      self.plane.devices[dim, step])

    def send(self, i, j, index, dim, step):
        copy = self.copy(i, j, index, dim, step)
        copy.start()
        self.started.append(copy)

    def await_first(self, index):
        self.copy((-1, 1, 2)[index], 0, index, self.dims[0], 1).wait_recv()

    def await_second(self, k, index):
        self.copy(OFFSETS[k], (-1, 1, 2)[index], 3 + 3 * k + index, self.dims[1], 1).wait_recv()

    def out_first(self):
        self.send(0, 0, 0, self.dims[0], 1)
        self.send(0, 0, 1, self.dims[0], -1)
        if "first" in self.opposite:
            self.send(0, 0, 2, self.dims[0], 2)

    def out_second(self, k):
        self.send(OFFSETS[k], 0, 3 + 3 * k, self.dims[1], 1)
        self.send(OFFSETS[k], 0, 4 + 3 * k, self.dims[1], -1)
        if k in self.opposite:
            self.send(OFFSETS[k], 0, 5 + 3 * k, self.dims[1], 2)

    def on_first(self):
        way = 1 if self.unit % 2 == 0 else -1
        order = ((0, -1, 1), (1, 1, 2)) if way == 1 else ((1, 1, 2), (0, -1, 1))
        for turn, (index, i, k) in enumerate(order):
            self.await_first(index)
            if turn == 0 and "first" not in self.opposite:
                self.send(i, 0, 2, self.dims[0], way)
            self.out_second(k)

    def far_first(self):
        self.await_first(2)
        self.out_second(3)

    def on_second(self, k):
        way = 1 if (self.unit + k) % 2 == 1 else -1
        order = (0, 1) if way == 1 else (1, 0)
        for turn, index in enumerate(order):
            self.await_second(k, index)
            if turn == 0 and k not in self.opposite:
                self.send(OFFSETS[k], -way, 5 + 3 * k, self.dims[1], way)

    def far_second(self, k):
        self.await_second(k, 2)

    def finish(self):
        for copy in self.started:
            copy.wait_send()


def run_units(units, multiply, between=()):
    between = list(between)
    half = len(units) // 2
    groups = [units[:half], units[half:]]

    def each(act, *args):
        for at in range(half):
            for group in groups:
                act(group[at], *args)

    def product(blocks):
        for group in groups:
            for unit in group:
                multiply([unit], blocks)

    def aside():
        if between:
            between.pop(0)()

    each(Gather.out_first)
    each(Gather.out_second, 0)
    aside()
    product([(0, 0)])
    each(Gather.on_first)
    aside()
    product([(-1, 0), (1, 0)])
    each(Gather.on_second, 0)
    each(Gather.far_first)
    aside()
    product([(0, -1), (0, 1), (2, 0)])
    aside()
    for k in (1, 2):
        each(Gather.on_second, k)
    product([(i, j) for i in (-1, 1) for j in (-1, 1)])
    aside()
    each(Gather.on_second, 3)
    product([(2, -1), (2, 1)])
    aside()
    for k in range(SIDE - 1):
        each(Gather.far_second, k)
        product([(OFFSETS[k], 2)])
        aside()
    for at in range(half):
        for group in groups:
            group[at].far_second(SIDE - 1)
            multiply([group[at]], [(OFFSETS[SIDE - 1], 2)])


class PlaneSum:
    def __init__(self, plane, own, column, line, sent, landed):
        self.plane, self.boxes, self.sent, self.landed = plane, (column, line), sent, landed
        self.sources, self.copies = (own, line.at[3]), []

    def start(self, turn):
        for at, step in enumerate((1, -1, 2)):
            index = 3 * turn + at
            copy = remote(self.sources[turn], self.boxes[turn].at[at], self.sent.at[index], self.landed.at[index],
                          self.plane.devices["yx"[turn], step])
            copy.start()
            self.copies.append(copy)

    def total(self, turn):
        for copy in self.copies[3 * turn :]:
            copy.wait_recv()
        box = self.boxes[turn]
        return self.sources[turn][...] + box[0] + box[1] + box[2]

    def pass_on(self):
        self.boxes[1][3] = self.total(0)
        self.start(1)

    def finish(self):
        for copy in self.copies:
            copy.wait_send()


def make_units(plane, buf, sent, landed, rows, count, opposite):
    size = rows // count
    return [
        Gather(plane, buf, sent, landed, u, u * size, size, "yx" if u < count // 2 else "xy", opposite)
        for u in range(count)
    ]


SPAN = 4
NORM_ROWS = 16
IN_UNITS, OUT_UNITS = 4, 2
FACTOR = float(HD ** -0.5 * 1.4426950408889634)


def feat(u):
    return jnp.where(u > 0, u + 1.0, jnp.exp(jnp.minimum(u, 0.0)))


def product_of(buf, w_ref, acc, finish=None):
    begun, seen = set(), {}

    def multiply(units, blocks):
        at = pl.ds(units[0].lo, sum(unit.rows for unit in units))
        key = tuple(unit.unit for unit in units)
        total = acc[at] if begun.issuperset(key) else None
        for i, j in blocks:
            slot = units[0].slot(i, j)
            term = jnp.dot(buf[slot, at], w_ref[slot], preferred_element_type=F32)
            total = term if total is None else total + term
        begun.update(key)
        for one in key:
            seen[one] = seen.get(one, 0) + len(blocks)
        if finish is not None and seen[key[0]] == HEADS:
            finish(units[0], total)
        else:
            acc[at] = total

    return multiply


def layer_kernel(segments, gate_ref, tokens_hbm, gain_hbm, w_hbm, wo_hbm, o_ref,
                 tokens_ref, gain_ref, w_ref, wo_ref, buf, acc, own, column, line, spread, q_ref, kv, top_ref, sum_ref, local_ref,
                 term, parts, outgoing, incoming, share, memory, obuf, oacc,
                 ready, in_sem, g_sent, g_landed, n_sent, n_landed, kv_sent, kv_landed, a_sent, a_landed, b_sent, b_landed,
                 c_sent, c_landed, o_sent, o_landed):
    loads = [
        pltpu.make_async_copy(source, target, in_sem.at[at])
        for at, (source, target) in enumerate(
            ((tokens_hbm, tokens_ref), (gain_hbm, gain_ref), (w_hbm, w_ref), (wo_hbm, wo_ref))
        )
    ]
    for load in loads:
        load.start()
    plane = Plane()
    s, x, y = place()
    h = x * SIDE + y
    seg, pos = s // SPAN, s % SPAN
    base = seg * SPAN
    peers = {step: (base + lax.rem(pos + step, SPAN), h) for step in (1, 2, 3)}
    mate = (base + pos // 2 * 2 + 1 - pos % 2, h)
    mate_slot = pos // 2 * 2 + 1 - pos % 2
    across, across_slot = peers[2], lax.rem(pos + 2, SPAN)
    relayed_slot = lax.rem(mate_slot + 2, SPAN)
    later = [(lax.rem(s + SPAN * d, segments * SPAN), h) for d in range(1, segments)]
    partners = plane.neighbours() + [plane.devices["x", 2], plane.devices["y", 2]] + list(peers.values())
    barrier = pltpu.get_barrier_semaphore()
    for partner in partners:
        pl.semaphore_signal(barrier, inc=1, device_id=partner, device_id_type=MESH)

    for d in range(1, segments):
        @pl.when(seg + d < segments)
        def _():
            pl.semaphore_signal(barrier, inc=1, device_id=later[d - 1], device_id_type=MESH)

    loads[0].wait()
    loads[1].wait()
    values = tokens_ref[...].astype(F32)
    rows, width = values.shape
    buf[h] = (values * gain_ref[...].astype(F32)).astype(BF16)
    own[...] = lax.dot_general(
        jnp.ones((8, width), F32), values * values, (((1,), (1,)), ((), ())),
        precision=HIGH, preferred_element_type=F32,
    )
    pl.semaphore_wait(barrier, len(partners) + seg)

    squares = PlaneSum(plane, own, column, line, n_sent, n_landed)

    def scales():
        scale = lax.rsqrt(squares.total(1) / (width * HEADS) + EPS)
        pick = (lax.broadcasted_iota(jnp.int32, (8, HD), 0) == 0).astype(F32)
        spread[...] = lax.dot_general(
            scale, pick, (((0,), (0,)), ((), ())), precision=HIGH, preferred_element_type=F32
        )

    piece = HD // SPAN
    whole = []
    size = rows // IN_UNITS

    def over(slot, unit, to):
        ref = kv.at[slot, pl.ds(unit * size, size)]
        return remote(ref, ref, kv_sent.at[1 + unit], kv_landed.at[1 + unit], to)

    def relay(slot, unit):
        ref = kv.at[slot, pl.ds(unit * size, size)]
        at = 1 + IN_UNITS + unit
        return remote(ref, ref, kv_sent.at[at], kv_landed.at[at], mate)


    def finish_rows(unit, total):
        at = unit.at
        rscale = spread[at]
        key = (total[:, HD : 2 * HD] * rscale).astype(BF16)
        value = (total[:, 2 * HD :] * rscale).astype(BF16)
        kv[pos, at, :HD] = key
        kv[pos, at, HD:] = value
        key = feat(key.astype(F32))
        product = lax.dot_general(key.astype(BF16), value, (((0,), (0,)), ((), ())), preferred_element_type=F32)
        amount = jnp.sum(key, axis=0, keepdims=True)
        whole[:] = [whole[0] + product, whole[1] + amount] if whole else [product, amount]
        q_ref[at] = (total[:, :HD] * rscale).astype(BF16)

    def begin():
        squares.start(0)
        loads[2].wait()
        for d in range(1, segments):
            @pl.when(seg - d >= 0)
            def _():
                pl.semaphore_signal(ready.at[d - 1], inc=1, device_id=later[segments - d - 1], device_id_type=MESH)

    units = make_units(plane, buf, g_sent, g_landed, rows, IN_UNITS, ())
    run_units(units, product_of(buf, w_ref, acc, finish_rows), [begin, squares.pass_on, scales])

    to_mate = remote(kv.at[pos], kv.at[pos], kv_sent.at[0], kv_landed.at[0], mate)
    from_mate = remote(kv.at[mate_slot], kv.at[mate_slot], kv_sent.at[0], kv_landed.at[0], mate)

    for at in range(SPAN):
        term[at, :piece] = whole[0][at * piece : (at + 1) * piece].astype(BF16)
        term[at, piece:] = jnp.broadcast_to(whole[1], (NORM_ROWS, HD)).astype(BF16)
    first = []
    for step in (2, 1, 3):
        copy = remote(term.at[lax.rem(pos + step, SPAN)], parts.at[step - 1],
                      a_sent.at[step - 1], a_landed.at[step - 1], peers[step])
        copy.start()
        first.append(copy)

    @pl.when(pos < 2)
    def _():
        for unit in range(IN_UNITS):
            over(pos, unit, across).start()

    to_mate.start()

    chunk = 128

    def attend(slot, causal):
        for r in range(rows // chunk):
            at = pl.ds(r * chunk, chunk)
            live = (r + 1) * chunk if causal else rows
            scores = lax.dot_general(
                q_ref[at], kv[slot, :live, :HD], (((1,), (1,)), ((), ())), preferred_element_type=F32
            )
            if causal:
                row = lax.broadcasted_iota(jnp.int32, (chunk, live), 0) + r * chunk
                scores = jnp.where(row >= lax.broadcasted_iota(jnp.int32, (chunk, live), 1), scores, -1e30)
            top = jnp.max(scores, axis=1, keepdims=True)
            if not causal:
                before = top_ref[at]
                top = jnp.maximum(top, before)
                shrink = jnp.exp2((before - top) * FACTOR)
            expo = jnp.exp2((scores - top) * FACTOR)
            weight = jnp.sum(expo, axis=1, keepdims=True)
            mixed = jnp.dot(expo.astype(BF16), kv[slot, :live, HD:], preferred_element_type=F32)
            if not causal:
                weight = weight + sum_ref[at] * shrink
                mixed = mixed + local_ref[at] * shrink
            top_ref[at] = top
            sum_ref[at] = weight
            local_ref[at] = mixed

    attend(pos, True)

    for copy in first:
        copy.wait_recv()
    here = pl.ds(pl.multiple_of(pos * piece, 16), piece)
    total = term[pos].astype(F32)
    for at in range(3):
        total = total + parts[at].astype(F32)
    outgoing[...] = total.astype(BF16)

    def second(d):
        return remote(outgoing, incoming.at[d - 1], b_sent.at[d - 1], b_landed.at[d - 1], later[d - 1])

    order = sorted(range(1, segments), key=lambda d: -min(d, segments - d))
    for d in order:
        @pl.when(seg + d < segments)
        def _():
            pl.semaphore_wait(ready.at[d - 1], 1)
            second(d).start()

    from_mate.wait_recv()

    @pl.when(mate_slot < pos)
    def _():
        attend(mate_slot, False)

    @pl.when(pos >= 2)
    def _():
        for unit in range(IN_UNITS):
            over(across_slot, unit, across).wait_recv()
            relay(across_slot, unit).start()

    queries = feat(q_ref[...].astype(F32)).astype(BF16)

    share[...] = jnp.zeros_like(share)
    for d in reversed(order):
        @pl.when(seg - d >= 0)
        def _():
            second(d).wait_recv()
            share[...] += incoming[d - 1].astype(F32)
    def third(step):
        return remote(memory.at[here], memory.at[here], c_sent.at[step - 1], c_landed.at[step - 1], peers[step])

    @pl.when(seg == 0)
    def _():
        memory[...] = jnp.zeros_like(memory)

    @pl.when(seg > 0)
    def _():
        memory[here] = share[:piece].astype(BF16)
        for step in (2, 1, 3):
            third(step).start()

    @pl.when(pos >= 2)
    def _():
        attend(across_slot, False)
        for unit in range(IN_UNITS):
            relay(relayed_slot, unit).wait_recv()
        attend(relayed_slot, False)

    gate = jax.nn.sigmoid(jnp.full((1, HD), gate_ref[0], F32))
    local_ref[...] = local_ref[...] * ((1.0 - gate) / sum_ref[...])

    pick = (lax.broadcasted_iota(jnp.int32, (8, HD), 0) == 0).astype(F32)
    norm = lax.dot_general(
        share[piece : piece + 8], pick, (((0,), (0,)), ((), ())), precision=HIGH, preferred_element_type=F32
    )
    denom = jnp.dot(queries, norm.astype(BF16), preferred_element_type=F32)
    weight = gate / jnp.maximum(denom, 1.0)

    @pl.when(seg > 0)
    def _():
        for step in (1, 2, 3):
            there = memory.at[pl.ds(pl.multiple_of(lax.rem(pos + SPAN - step, SPAN) * piece, 16), piece)]
            remote(there, there, c_sent.at[step - 1], c_landed.at[step - 1], peers[step]).wait_recv()

    numer = jnp.dot(queries, memory[...], preferred_element_type=F32)
    obuf[h] = (numer * weight + local_ref[...]).astype(BF16)

    loads[3].wait()
    out_units = make_units(plane, obuf, o_sent, o_landed, rows, OUT_UNITS, ("first",))

    def finish(unit, total):
        o_ref[unit.at] = total.astype(BF16)

    run_units(out_units, product_of(obuf, wo_ref, oacc, finish))

    for unit in units + out_units:
        unit.finish()
    squares.finish()
    for copy in [to_mate] + first:
        copy.wait_send()

    @pl.when(seg > 0)
    def _():
        for step in (1, 2, 3):
            third(step).wait_send()

    @pl.when(pos < 2)
    def _():
        for unit in range(IN_UNITS):
            over(pos, unit, across).wait_send()

    @pl.when(pos >= 2)
    def _():
        for unit in range(IN_UNITS):
            relay(across_slot, unit).wait_send()

    for d in order:
        @pl.when(seg + d < segments)
        def _():
            second(d).wait_send()


def layer(gate, tokens, gain, weights, out_weights, segments):
    rows, width = tokens.shape
    columns, out_columns = weights.shape[2], out_weights.shape[2]
    piece = HD // SPAN
    anywhere = pl.BlockSpec(memory_space=pl.ANY)
    dma = pltpu.SemaphoreType.DMA
    return pl.pallas_call(
        functools.partial(layer_kernel, segments),
        out_shape=jax.ShapeDtypeStruct((rows, out_columns), BF16),
        in_specs=[pl.BlockSpec(memory_space=pltpu.SMEM)] + [anywhere] * 4,
        out_specs=pl.BlockSpec(memory_space=pltpu.VMEM),
        scratch_shapes=[
            pltpu.VMEM((rows, width), BF16),
            pltpu.VMEM((1, width), BF16),
            pltpu.VMEM((HEADS, width, columns), BF16),
            pltpu.VMEM((HEADS, HD, out_columns), BF16),
            pltpu.VMEM((HEADS, rows, width), BF16),
            pltpu.VMEM((rows, columns), F32),
            pltpu.VMEM((8, rows), F32),
            pltpu.VMEM((3, 8, rows), F32),
            pltpu.VMEM((4, 8, rows), F32),
            pltpu.VMEM((rows, HD), F32),
            pltpu.VMEM((rows, HD), BF16),
            pltpu.VMEM((SPAN, rows, 2 * HD), BF16),
            pltpu.VMEM((rows, 1), F32),
            pltpu.VMEM((rows, 1), F32),
            pltpu.VMEM((rows, HD), F32),
            pltpu.VMEM((SPAN, piece + NORM_ROWS, HD), BF16),
            pltpu.VMEM((3, piece + NORM_ROWS, HD), BF16),
            pltpu.VMEM((piece + NORM_ROWS, HD), BF16),
            pltpu.VMEM((segments - 1, piece + NORM_ROWS, HD), BF16),
            pltpu.VMEM((piece + NORM_ROWS, HD), F32),
            pltpu.VMEM((HD, HD), BF16),
            pltpu.VMEM((HEADS, rows, HD), BF16),
            pltpu.VMEM((rows, out_columns), F32),
            pltpu.SemaphoreType.REGULAR((segments - 1,)),
            dma((4,)),
            dma((IN_UNITS, 15)),
            dma((IN_UNITS, 15)),
            dma((6,)),
            dma((6,)),
            dma((1 + 2 * IN_UNITS,)),
            dma((1 + 2 * IN_UNITS,)),
            dma((3,)),
            dma((3,)),
            dma((segments - 1,)),
            dma((segments - 1,)),
            dma((3,)),
            dma((3,)),
            dma((OUT_UNITS, 15)),
            dma((OUT_UNITS, 15)),
        ],
        compiler_params=pltpu.CompilerParams(collective_id=0, has_side_effects=True, vmem_limit_bytes=56 << 20),
        name="layer",
    )(gate, tokens, gain, weights, out_weights)


def on_device(tokens, norm_gain, qkv_weight, out_weight, mem_gate):
    weights = qkv_weight.reshape(HEADS, tokens.shape[1], 3 * HD)
    out_weights = out_weight.reshape(HEADS, HD, out_weight.shape[1])
    return layer(mem_gate, tokens, norm_gain, weights, out_weights, lax.axis_size("seq") // SPAN)


def solution(mesh):
    placed = (P("seq", "head"), P(None, "head"), P(None, "head", None), P(None, "head"), P("head"))
    return jax.shard_map(
        on_device, mesh=mesh, in_specs=placed, out_specs=P("seq", "head"), check_vma=False
    )
```

```python
import functools

import jax
import jax.numpy as jnp
from jax import lax
from jax.experimental import pallas as pl
from jax.experimental.pallas import tpu as pltpu
from jax.sharding import PartitionSpec as P

SEG = 2048
EPS = 1e-06
SIDE = 4
HEADS = SIDE * SIDE
HD = 128
OFFSETS = (0, -1, 1, 2)
MESH = pl.DeviceIdType.MESH
HIGH = lax.Precision.HIGHEST
F32, BF16 = jnp.float32, jnp.bfloat16


def place():
    s, h = lax.axis_index("seq"), lax.axis_index("head")
    return s, h // SIDE, h % SIDE


def around(position, step):
    return lax.rem(position + step + SIDE, SIDE)


def remote(source, target, sent, landed, partner):
    return pltpu.make_async_remote_copy(
        src_ref=source, dst_ref=target, send_sem=sent, recv_sem=landed,
        device_id=partner, device_id_type=MESH,
    )


class Plane:
    def __init__(self):
        s, x, y = place()
        xs = {i: around(x, i) for i in OFFSETS}
        ys = {j: around(y, j) for j in OFFSETS}
        self.slots = {(i, j): xs[i] * SIDE + ys[j] for i in OFFSETS for j in OFFSETS}
        self.devices = {("x", i): (s, self.slots[i, 0]) for i in OFFSETS}
        self.devices.update({("y", j): (s, self.slots[0, j]) for j in OFFSETS})

    def neighbours(self):
        return [self.devices[dim, step] for dim in "xy" for step in (1, -1)]


class Gather:
    def __init__(self, plane, buf, sent, landed, unit, first_row, rows, dims, opposite):
        self.plane, self.buf, self.sent, self.landed, self.unit = plane, buf, sent, landed, unit
        self.lo, self.rows, self.dims, self.opposite = first_row, rows, dims, opposite
        self.at = pl.ds(first_row, rows)
        self.started = []

    def slot(self, i, j):
        return self.plane.slots[(i, j) if self.dims == "xy" else (j, i)]

    def copy(self, i, j, index, dim, step):
        ref = self.buf.at[self.slot(i, j), self.at]
        return remote(ref, ref, self.sent.at[self.unit, index], self.landed.at[self.unit, index],
                      self.plane.devices[dim, step])

    def send(self, i, j, index, dim, step):
        copy = self.copy(i, j, index, dim, step)
        copy.start()
        self.started.append(copy)

    def await_first(self, index):
        self.copy((-1, 1, 2)[index], 0, index, self.dims[0], 1).wait_recv()

    def await_second(self, k, index):
        self.copy(OFFSETS[k], (-1, 1, 2)[index], 3 + 3 * k + index, self.dims[1], 1).wait_recv()

    def out_first(self):
        self.send(0, 0, 0, self.dims[0], 1)
        self.send(0, 0, 1, self.dims[0], -1)
        if "first" in self.opposite:
            self.send(0, 0, 2, self.dims[0], 2)

    def out_second(self, k):
        self.send(OFFSETS[k], 0, 3 + 3 * k, self.dims[1], 1)
        self.send(OFFSETS[k], 0, 4 + 3 * k, self.dims[1], -1)
        if k in self.opposite:
            self.send(OFFSETS[k], 0, 5 + 3 * k, self.dims[1], 2)

    def on_first(self):
        way = 1 if self.unit % 2 == 0 else -1
        order = ((0, -1, 1), (1, 1, 2)) if way == 1 else ((1, 1, 2), (0, -1, 1))
        for turn, (index, i, k) in enumerate(order):
            self.await_first(index)
            if turn == 0 and "first" not in self.opposite:
                self.send(i, 0, 2, self.dims[0], way)
            self.out_second(k)

    def far_first(self):
        self.await_first(2)
        self.out_second(3)

    def on_second(self, k):
        way = 1 if (self.unit + k) % 2 == 1 else -1
        order = (0, 1) if way == 1 else (1, 0)
        for turn, index in enumerate(order):
            self.await_second(k, index)
            if turn == 0 and k not in self.opposite:
                self.send(OFFSETS[k], -way, 5 + 3 * k, self.dims[1], way)

    def far_second(self, k):
        self.await_second(k, 2)

    def finish(self):
        for copy in self.started:
            copy.wait_send()


def run_units(units, multiply, between=()):
    between = list(between)
    half = len(units) // 2
    groups = [units[:half], units[half:]]

    def each(act, *args):
        for at in range(half):
            for group in groups:
                act(group[at], *args)

    def product(blocks):
        for group in groups:
            for unit in group:
                multiply([unit], blocks)

    def aside():
        if between:
            between.pop(0)()

    each(Gather.out_first)
    each(Gather.out_second, 0)
    aside()
    product([(0, 0)])
    each(Gather.on_first)
    aside()
    product([(-1, 0), (1, 0)])
    each(Gather.on_second, 0)
    each(Gather.far_first)
    aside()
    product([(0, -1), (0, 1), (2, 0)])
    aside()
    for k in (1, 2):
        each(Gather.on_second, k)
    product([(i, j) for i in (-1, 1) for j in (-1, 1)])
    aside()
    each(Gather.on_second, 3)
    product([(2, -1), (2, 1)])
    aside()
    for k in range(SIDE - 1):
        each(Gather.far_second, k)
        product([(OFFSETS[k], 2)])
        aside()
    for at in range(half):
        for group in groups:
            group[at].far_second(SIDE - 1)
            multiply([group[at]], [(OFFSETS[SIDE - 1], 2)])


class PlaneSum:
    def __init__(self, plane, own, column, line, sent, landed):
        self.plane, self.boxes, self.sent, self.landed = plane, (column, line), sent, landed
        self.sources, self.copies = (own, line.at[3]), []

    def start(self, turn):
        for at, step in enumerate((1, -1, 2)):
            index = 3 * turn + at
            copy = remote(self.sources[turn], self.boxes[turn].at[at], self.sent.at[index], self.landed.at[index],
                          self.plane.devices["yx"[turn], step])
            copy.start()
            self.copies.append(copy)

    def total(self, turn):
        for copy in self.copies[3 * turn :]:
            copy.wait_recv()
        box = self.boxes[turn]
        return self.sources[turn][...] + box[0] + box[1] + box[2]

    def pass_on(self):
        self.boxes[1][3] = self.total(0)
        self.start(1)

    def finish(self):
        for copy in self.copies:
            copy.wait_send()


def make_units(plane, buf, sent, landed, rows, count, opposite):
    size = rows // count
    return [
        Gather(plane, buf, sent, landed, u, u * size, size, "yx" if u < count // 2 else "xy", opposite)
        for u in range(count)
    ]


SPAN = 4
NORM_ROWS = 16
IN_UNITS, OUT_UNITS = 4, 2
FACTOR = float(HD ** -0.5 * 1.4426950408889634)


def feat(u):
    return jnp.where(u > 0, u + 1.0, jnp.exp(jnp.minimum(u, 0.0)))


def product_of(buf, w_ref, acc, finish=None):
    begun, seen = set(), {}

    def multiply(units, blocks):
        at = pl.ds(units[0].lo, sum(unit.rows for unit in units))
        key = tuple(unit.unit for unit in units)
        total = acc[at] if begun.issuperset(key) else None
        for i, j in blocks:
            slot = units[0].slot(i, j)
            term = jnp.dot(buf[slot, at], w_ref[slot], preferred_element_type=F32)
            total = term if total is None else total + term
        begun.update(key)
        for one in key:
            seen[one] = seen.get(one, 0) + len(blocks)
        if finish is not None and seen[key[0]] == HEADS:
            finish(units[0], total)
        else:
            acc[at] = total

    return multiply


def layer_kernel(segments, gate_ref, tokens_hbm, gain_hbm, w_hbm, wo_hbm, o_ref,
                 tokens_ref, gain_ref, w_ref, wo_ref, buf, acc, own, column, line, spread, q_ref, kv, top_ref, sum_ref, local_ref,
                 term, parts, outgoing, incoming, share, memory, obuf, oacc,
                 ready, in_sem, g_sent, g_landed, n_sent, n_landed, kv_sent, kv_landed, a_sent, a_landed, b_sent, b_landed,
                 c_sent, c_landed, o_sent, o_landed):
    loads = [
        pltpu.make_async_copy(source, target, in_sem.at[at])
        for at, (source, target) in enumerate(
            ((tokens_hbm, tokens_ref), (gain_hbm, gain_ref), (w_hbm, w_ref), (wo_hbm, wo_ref))
        )
    ]
    for load in loads:
        load.start()
    plane = Plane()
    s, x, y = place()
    h = x * SIDE + y
    seg, pos = s // SPAN, s % SPAN
    base = seg * SPAN
    peers = {step: (base + lax.rem(pos + step, SPAN), h) for step in (1, 2, 3)}
    mate = (base + pos // 2 * 2 + 1 - pos % 2, h)
    mate_slot = pos // 2 * 2 + 1 - pos % 2
    across, across_slot = peers[2], lax.rem(pos + 2, SPAN)
    relayed_slot = lax.rem(mate_slot + 2, SPAN)
    later = [(lax.rem(s + SPAN * d, segments * SPAN), h) for d in range(1, segments)]
    partners = plane.neighbours() + [plane.devices["x", 2], plane.devices["y", 2]] + list(peers.values())
    barrier = pltpu.get_barrier_semaphore()
    for partner in partners:
        pl.semaphore_signal(barrier, inc=1, device_id=partner, device_id_type=MESH)

    for d in range(1, segments):
        @pl.when(seg + d < segments)
        def _():
            pl.semaphore_signal(barrier, inc=1, device_id=later[d - 1], device_id_type=MESH)

    loads[0].wait()
    loads[1].wait()
    values = tokens_ref[...].astype(F32)
    rows, width = values.shape
    buf[h] = (values * gain_ref[...].astype(F32)).astype(BF16)
    own[...] = lax.dot_general(
        jnp.ones((8, width), F32), values * values, (((1,), (1,)), ((), ())),
        precision=HIGH, preferred_element_type=F32,
    )
    pl.semaphore_wait(barrier, len(partners) + seg)

    squares = PlaneSum(plane, own, column, line, n_sent, n_landed)

    def scales():
        scale = lax.rsqrt(squares.total(1) / (width * HEADS) + EPS)
        pick = (lax.broadcasted_iota(jnp.int32, (8, HD), 0) == 0).astype(F32)
        spread[...] = lax.dot_general(
            scale, pick, (((0,), (0,)), ((), ())), precision=HIGH, preferred_element_type=F32
        )

    piece = HD // SPAN
    whole = []
    size = rows // IN_UNITS

    def over(slot, unit, to):
        ref = kv.at[slot, pl.ds(unit * size, size)]
        return remote(ref, ref, kv_sent.at[1 + unit], kv_landed.at[1 + unit], to)

    def relay(slot, unit):
        ref = kv.at[slot, pl.ds(unit * size, size)]
        at = 1 + IN_UNITS + unit
        return remote(ref, ref, kv_sent.at[at], kv_landed.at[at], mate)


    def finish_rows(unit, total):
        at = unit.at
        rscale = spread[at]
        key = (total[:, HD : 2 * HD] * rscale).astype(BF16)
        value = (total[:, 2 * HD :] * rscale).astype(BF16)
        kv[pos, at, :HD] = key
        kv[pos, at, HD:] = value
        key = feat(key.astype(F32))
        product = lax.dot_general(key.astype(BF16), value, (((0,), (0,)), ((), ())), preferred_element_type=F32)
        amount = jnp.sum(key, axis=0, keepdims=True)
        whole[:] = [whole[0] + product, whole[1] + amount] if whole else [product, amount]
        q_ref[at] = (total[:, :HD] * rscale).astype(BF16)

    def begin():
        squares.start(0)
        loads[2].wait()
        for d in range(1, segments):
            @pl.when(seg - d >= 0)
            def _():
                pl.semaphore_signal(ready.at[d - 1], inc=1, device_id=later[segments - d - 1], device_id_type=MESH)

    units = make_units(plane, buf, g_sent, g_landed, rows, IN_UNITS, ())
    run_units(units, product_of(buf, w_ref, acc, finish_rows), [begin, squares.pass_on, scales])

    to_mate = remote(kv.at[pos], kv.at[pos], kv_sent.at[0], kv_landed.at[0], mate)
    from_mate = remote(kv.at[mate_slot], kv.at[mate_slot], kv_sent.at[0], kv_landed.at[0], mate)

    for at in range(SPAN):
        term[at, :piece] = whole[0][at * piece : (at + 1) * piece].astype(BF16)
        term[at, piece:] = jnp.broadcast_to(whole[1], (NORM_ROWS, HD)).astype(BF16)
    first = []
    for step in (2, 1, 3):
        copy = remote(term.at[lax.rem(pos + step, SPAN)], parts.at[step - 1],
                      a_sent.at[step - 1], a_landed.at[step - 1], peers[step])
        copy.start()
        first.append(copy)

    @pl.when(pos < 2)
    def _():
        for unit in range(IN_UNITS // 2):
            over(pos, unit, across).start()

    to_mate.start()

    chunk = 128

    def attend(slot, causal):
        for r in range(rows // chunk):
            at = pl.ds(r * chunk, chunk)
            live = (r + 1) * chunk if causal else rows
            scores = lax.dot_general(
                q_ref[at], kv[slot, :live, :HD], (((1,), (1,)), ((), ())), preferred_element_type=F32
            )
            if causal:
                row = lax.broadcasted_iota(jnp.int32, (chunk, live), 0) + r * chunk
                scores = jnp.where(row >= lax.broadcasted_iota(jnp.int32, (chunk, live), 1), scores, -1e30)
            top = jnp.max(scores, axis=1, keepdims=True)
            if not causal:
                before = top_ref[at]
                top = jnp.maximum(top, before)
                shrink = jnp.exp2((before - top) * FACTOR)
            expo = jnp.exp2((scores - top) * FACTOR)
            weight = jnp.sum(expo, axis=1, keepdims=True)
            mixed = jnp.dot(expo.astype(BF16), kv[slot, :live, HD:], preferred_element_type=F32)
            if not causal:
                weight = weight + sum_ref[at] * shrink
                mixed = mixed + local_ref[at] * shrink
            top_ref[at] = top
            sum_ref[at] = weight
            local_ref[at] = mixed

    attend(pos, True)

    for copy in first:
        copy.wait_recv()
    here = pl.ds(pl.multiple_of(pos * piece, 16), piece)
    total = term[pos].astype(F32)
    for at in range(3):
        total = total + parts[at].astype(F32)
    outgoing[...] = total.astype(BF16)

    def second(d):
        return remote(outgoing, incoming.at[d - 1], b_sent.at[d - 1], b_landed.at[d - 1], later[d - 1])

    order = sorted(range(1, segments), key=lambda d: -min(d, segments - d))
    for d in order:
        @pl.when(seg + d < segments)
        def _():
            pl.semaphore_wait(ready.at[d - 1], 1)
            second(d).start()

    @pl.when(pos < 2)
    def _():
        for unit in range(IN_UNITS // 2, IN_UNITS):
            over(pos, unit, across).start()

    from_mate.wait_recv()

    @pl.when(mate_slot < pos)
    def _():
        attend(mate_slot, False)

    @pl.when(pos >= 2)
    def _():
        for unit in range(IN_UNITS):
            over(across_slot, unit, across).wait_recv()
            relay(across_slot, unit).start()

    queries = feat(q_ref[...].astype(F32)).astype(BF16)

    share[...] = jnp.zeros_like(share)
    for d in reversed(order):
        @pl.when(seg - d >= 0)
        def _():
            second(d).wait_recv()
            share[...] += incoming[d - 1].astype(F32)
    def third(step):
        return remote(memory.at[here], memory.at[here], c_sent.at[step - 1], c_landed.at[step - 1], peers[step])

    @pl.when(seg == 0)
    def _():
        memory[...] = jnp.zeros_like(memory)

    @pl.when(seg > 0)
    def _():
        memory[here] = share[:piece].astype(BF16)
        for step in (2, 1, 3):
            third(step).start()

    @pl.when(pos >= 2)
    def _():
        attend(across_slot, False)
        for unit in range(IN_UNITS):
            relay(relayed_slot, unit).wait_recv()
        attend(relayed_slot, False)

    gate = jax.nn.sigmoid(jnp.full((1, HD), gate_ref[0], F32))
    local_ref[...] = local_ref[...] * ((1.0 - gate) / sum_ref[...])

    pick = (lax.broadcasted_iota(jnp.int32, (8, HD), 0) == 0).astype(F32)
    norm = lax.dot_general(
        share[piece : piece + 8], pick, (((0,), (0,)), ((), ())), precision=HIGH, preferred_element_type=F32
    )
    denom = jnp.dot(queries, norm.astype(BF16), preferred_element_type=F32)
    weight = gate / jnp.maximum(denom, 1.0)

    @pl.when(seg > 0)
    def _():
        for step in (1, 2, 3):
            there = memory.at[pl.ds(pl.multiple_of(lax.rem(pos + SPAN - step, SPAN) * piece, 16), piece)]
            remote(there, there, c_sent.at[step - 1], c_landed.at[step - 1], peers[step]).wait_recv()

    numer = jnp.dot(queries, memory[...], preferred_element_type=F32)
    obuf[h] = (numer * weight + local_ref[...]).astype(BF16)

    loads[3].wait()
    out_units = make_units(plane, obuf, o_sent, o_landed, rows, OUT_UNITS, ("first",))

    def finish(unit, total):
        o_ref[unit.at] = total.astype(BF16)

    run_units(out_units, product_of(obuf, wo_ref, oacc, finish))

    for unit in units + out_units:
        unit.finish()
    squares.finish()
    for copy in [to_mate] + first:
        copy.wait_send()

    @pl.when(seg > 0)
    def _():
        for step in (1, 2, 3):
            third(step).wait_send()

    @pl.when(pos < 2)
    def _():
        for unit in range(IN_UNITS):
            over(pos, unit, across).wait_send()

    @pl.when(pos >= 2)
    def _():
        for unit in range(IN_UNITS):
            relay(across_slot, unit).wait_send()

    for d in order:
        @pl.when(seg + d < segments)
        def _():
            second(d).wait_send()


def layer(gate, tokens, gain, weights, out_weights, segments):
    rows, width = tokens.shape
    columns, out_columns = weights.shape[2], out_weights.shape[2]
    piece = HD // SPAN
    anywhere = pl.BlockSpec(memory_space=pl.ANY)
    dma = pltpu.SemaphoreType.DMA
    return pl.pallas_call(
        functools.partial(layer_kernel, segments),
        out_shape=jax.ShapeDtypeStruct((rows, out_columns), BF16),
        in_specs=[pl.BlockSpec(memory_space=pltpu.SMEM)] + [anywhere] * 4,
        out_specs=pl.BlockSpec(memory_space=pltpu.VMEM),
        scratch_shapes=[
            pltpu.VMEM((rows, width), BF16),
            pltpu.VMEM((1, width), BF16),
            pltpu.VMEM((HEADS, width, columns), BF16),
            pltpu.VMEM((HEADS, HD, out_columns), BF16),
            pltpu.VMEM((HEADS, rows, width), BF16),
            pltpu.VMEM((rows, columns), F32),
            pltpu.VMEM((8, rows), F32),
            pltpu.VMEM((3, 8, rows), F32),
            pltpu.VMEM((4, 8, rows), F32),
            pltpu.VMEM((rows, HD), F32),
            pltpu.VMEM((rows, HD), BF16),
            pltpu.VMEM((SPAN, rows, 2 * HD), BF16),
            pltpu.VMEM((rows, 1), F32),
            pltpu.VMEM((rows, 1), F32),
            pltpu.VMEM((rows, HD), F32),
            pltpu.VMEM((SPAN, piece + NORM_ROWS, HD), BF16),
            pltpu.VMEM((3, piece + NORM_ROWS, HD), BF16),
            pltpu.VMEM((piece + NORM_ROWS, HD), BF16),
            pltpu.VMEM((segments - 1, piece + NORM_ROWS, HD), BF16),
            pltpu.VMEM((piece + NORM_ROWS, HD), F32),
            pltpu.VMEM((HD, HD), BF16),
            pltpu.VMEM((HEADS, rows, HD), BF16),
            pltpu.VMEM((rows, out_columns), F32),
            pltpu.SemaphoreType.REGULAR((segments - 1,)),
            dma((4,)),
            dma((IN_UNITS, 15)),
            dma((IN_UNITS, 15)),
            dma((6,)),
            dma((6,)),
            dma((1 + 2 * IN_UNITS,)),
            dma((1 + 2 * IN_UNITS,)),
            dma((3,)),
            dma((3,)),
            dma((segments - 1,)),
            dma((segments - 1,)),
            dma((3,)),
            dma((3,)),
            dma((OUT_UNITS, 15)),
            dma((OUT_UNITS, 15)),
        ],
        compiler_params=pltpu.CompilerParams(collective_id=0, has_side_effects=True, vmem_limit_bytes=56 << 20),
        name="layer",
    )(gate, tokens, gain, weights, out_weights)


def on_device(tokens, norm_gain, qkv_weight, out_weight, mem_gate):
    weights = qkv_weight.reshape(HEADS, tokens.shape[1], 3 * HD)
    out_weights = out_weight.reshape(HEADS, HD, out_weight.shape[1])
    return layer(mem_gate, tokens, norm_gain, weights, out_weights, lax.axis_size("seq") // SPAN)


def solution(mesh):
    placed = (P("seq", "head"), P(None, "head"), P(None, "head", None), P(None, "head"), P("head"))
    return jax.shard_map(
        on_device, mesh=mesh, in_specs=placed, out_specs=P("seq", "head"), check_vma=False
    )
```

```python
import functools

import jax
import jax.numpy as jnp
from jax import lax
from jax.experimental import pallas as pl
from jax.experimental.pallas import tpu as pltpu
from jax.sharding import PartitionSpec as P

SEG = 2048
EPS = 1e-06
SIDE = 4
HEADS = SIDE * SIDE
HD = 128
OFFSETS = (0, -1, 1, 2)
MESH = pl.DeviceIdType.MESH
HIGH = lax.Precision.HIGHEST
F32, BF16 = jnp.float32, jnp.bfloat16


def place():
    s, h = lax.axis_index("seq"), lax.axis_index("head")
    return s, h // SIDE, h % SIDE


def around(position, step):
    return lax.rem(position + step + SIDE, SIDE)


def remote(source, target, sent, landed, partner):
    return pltpu.make_async_remote_copy(
        src_ref=source, dst_ref=target, send_sem=sent, recv_sem=landed,
        device_id=partner, device_id_type=MESH,
    )


class Plane:
    def __init__(self):
        s, x, y = place()
        xs = {i: around(x, i) for i in OFFSETS}
        ys = {j: around(y, j) for j in OFFSETS}
        self.slots = {(i, j): xs[i] * SIDE + ys[j] for i in OFFSETS for j in OFFSETS}
        self.devices = {("x", i): (s, self.slots[i, 0]) for i in OFFSETS}
        self.devices.update({("y", j): (s, self.slots[0, j]) for j in OFFSETS})

    def neighbours(self):
        return [self.devices[dim, step] for dim in "xy" for step in (1, -1)]


class Gather:
    def __init__(self, plane, buf, sent, landed, unit, first_row, rows, dims, opposite):
        self.plane, self.buf, self.sent, self.landed, self.unit = plane, buf, sent, landed, unit
        self.lo, self.rows, self.dims, self.opposite = first_row, rows, dims, opposite
        self.at = pl.ds(first_row, rows)
        self.started = []

    def slot(self, i, j):
        return self.plane.slots[(i, j) if self.dims == "xy" else (j, i)]

    def copy(self, i, j, index, dim, step):
        ref = self.buf.at[self.slot(i, j), self.at]
        return remote(ref, ref, self.sent.at[self.unit, index], self.landed.at[self.unit, index],
                      self.plane.devices[dim, step])

    def send(self, i, j, index, dim, step):
        copy = self.copy(i, j, index, dim, step)
        copy.start()
        self.started.append(copy)

    def await_first(self, index):
        self.copy((-1, 1, 2)[index], 0, index, self.dims[0], 1).wait_recv()

    def await_second(self, k, index):
        self.copy(OFFSETS[k], (-1, 1, 2)[index], 3 + 3 * k + index, self.dims[1], 1).wait_recv()

    def out_first(self):
        self.send(0, 0, 0, self.dims[0], 1)
        self.send(0, 0, 1, self.dims[0], -1)
        if "first" in self.opposite:
            self.send(0, 0, 2, self.dims[0], 2)

    def out_second(self, k):
        self.send(OFFSETS[k], 0, 3 + 3 * k, self.dims[1], 1)
        self.send(OFFSETS[k], 0, 4 + 3 * k, self.dims[1], -1)
        if k in self.opposite:
            self.send(OFFSETS[k], 0, 5 + 3 * k, self.dims[1], 2)

    def on_first(self):
        way = 1 if self.unit % 2 == 0 else -1
        order = ((0, -1, 1), (1, 1, 2)) if way == 1 else ((1, 1, 2), (0, -1, 1))
        for turn, (index, i, k) in enumerate(order):
            self.await_first(index)
            if turn == 0 and "first" not in self.opposite:
                self.send(i, 0, 2, self.dims[0], way)
            self.out_second(k)

    def far_first(self):
        self.await_first(2)
        self.out_second(3)

    def on_second(self, k):
        way = 1 if (self.unit + k) % 2 == 1 else -1
        order = (0, 1) if way == 1 else (1, 0)
        for turn, index in enumerate(order):
            self.await_second(k, index)
            if turn == 0 and k not in self.opposite:
                self.send(OFFSETS[k], -way, 5 + 3 * k, self.dims[1], way)

    def far_second(self, k):
        self.await_second(k, 2)

    def finish(self):
        for copy in self.started:
            copy.wait_send()


def run_units(units, multiply, between=()):
    between = list(between)
    half = len(units) // 2
    groups = [units[:half], units[half:]]

    def each(act, *args):
        for at in range(half):
            for group in groups:
                act(group[at], *args)

    def product(blocks):
        for group in groups:
            for unit in group:
                multiply([unit], blocks)

    def aside():
        if between:
            between.pop(0)()

    each(Gather.out_first)
    each(Gather.out_second, 0)
    aside()
    product([(0, 0)])
    each(Gather.on_first)
    aside()
    product([(-1, 0), (1, 0)])
    each(Gather.on_second, 0)
    each(Gather.far_first)
    aside()
    product([(0, -1), (0, 1), (2, 0)])
    aside()
    for k in (1, 2):
        each(Gather.on_second, k)
    product([(i, j) for i in (-1, 1) for j in (-1, 1)])
    aside()
    each(Gather.on_second, 3)
    product([(2, -1), (2, 1)])
    aside()
    for k in range(SIDE - 1):
        each(Gather.far_second, k)
        product([(OFFSETS[k], 2)])
        aside()
    for at in range(half):
        for group in groups:
            group[at].far_second(SIDE - 1)
            multiply([group[at]], [(OFFSETS[SIDE - 1], 2)])


class PlaneSum:
    def __init__(self, plane, own, column, line, sent, landed):
        self.plane, self.boxes, self.sent, self.landed = plane, (column, line), sent, landed
        self.sources, self.copies = (own, line.at[3]), []

    def start(self, turn):
        for at, step in enumerate((1, -1, 2)):
            index = 3 * turn + at
            copy = remote(self.sources[turn], self.boxes[turn].at[at], self.sent.at[index], self.landed.at[index],
                          self.plane.devices["yx"[turn], step])
            copy.start()
            self.copies.append(copy)

    def total(self, turn):
        for copy in self.copies[3 * turn :]:
            copy.wait_recv()
        box = self.boxes[turn]
        return self.sources[turn][...] + box[0] + box[1] + box[2]

    def pass_on(self):
        self.boxes[1][3] = self.total(0)
        self.start(1)

    def finish(self):
        for copy in self.copies:
            copy.wait_send()


def make_units(plane, buf, sent, landed, rows, count, opposite):
    size = rows // count
    return [
        Gather(plane, buf, sent, landed, u, u * size, size, "yx" if u < count // 2 else "xy", opposite)
        for u in range(count)
    ]


SPAN = 4
NORM_ROWS = 16
IN_UNITS, OUT_UNITS = 4, 2
FACTOR = float(HD ** -0.5 * 1.4426950408889634)


def feat(u):
    return jnp.where(u > 0, u + 1.0, jnp.exp(jnp.minimum(u, 0.0)))


def product_of(buf, w_ref, acc, finish=None):
    begun, seen = set(), {}

    def multiply(units, blocks):
        at = pl.ds(units[0].lo, sum(unit.rows for unit in units))
        key = tuple(unit.unit for unit in units)
        total = acc[at] if begun.issuperset(key) else None
        for i, j in blocks:
            slot = units[0].slot(i, j)
            term = jnp.dot(buf[slot, at], w_ref[slot], preferred_element_type=F32)
            total = term if total is None else total + term
        begun.update(key)
        for one in key:
            seen[one] = seen.get(one, 0) + len(blocks)
        if finish is not None and seen[key[0]] == HEADS:
            finish(units[0], total)
        else:
            acc[at] = total

    return multiply


def layer_kernel(segments, gate_ref, tokens_hbm, gain_hbm, w_hbm, wo_hbm, o_ref,
                 tokens_ref, gain_ref, w_ref, wo_ref, buf, acc, own, column, line, spread, q_ref, kv, top_ref, sum_ref, local_ref,
                 term, parts, outgoing, incoming, share, memory, obuf, oacc,
                 ready, in_sem, g_sent, g_landed, n_sent, n_landed, kv_sent, kv_landed, a_sent, a_landed, b_sent, b_landed,
                 c_sent, c_landed, o_sent, o_landed):
    loads = [
        pltpu.make_async_copy(source, target, in_sem.at[at])
        for at, (source, target) in enumerate(
            ((tokens_hbm, tokens_ref), (gain_hbm, gain_ref), (w_hbm, w_ref), (wo_hbm, wo_ref))
        )
    ]
    for load in loads:
        load.start()
    plane = Plane()
    s, x, y = place()
    h = x * SIDE + y
    seg, pos = s // SPAN, s % SPAN
    base = seg * SPAN
    peers = {step: (base + lax.rem(pos + step, SPAN), h) for step in (1, 2, 3)}
    mate = (base + pos // 2 * 2 + 1 - pos % 2, h)
    mate_slot = pos // 2 * 2 + 1 - pos % 2
    across, across_slot = peers[2], lax.rem(pos + 2, SPAN)
    relayed_slot = lax.rem(mate_slot + 2, SPAN)
    later = [(lax.rem(s + SPAN * d, segments * SPAN), h) for d in range(1, segments)]
    partners = plane.neighbours() + [plane.devices["x", 2], plane.devices["y", 2]] + list(peers.values())
    barrier = pltpu.get_barrier_semaphore()
    for partner in partners:
        pl.semaphore_signal(barrier, inc=1, device_id=partner, device_id_type=MESH)

    for d in range(1, segments):
        @pl.when(seg + d < segments)
        def _():
            pl.semaphore_signal(barrier, inc=1, device_id=later[d - 1], device_id_type=MESH)

    loads[0].wait()
    loads[1].wait()
    values = tokens_ref[...].astype(F32)
    rows, width = values.shape
    buf[h] = (values * gain_ref[...].astype(F32)).astype(BF16)
    own[...] = lax.dot_general(
        jnp.ones((8, width), F32), values * values, (((1,), (1,)), ((), ())),
        precision=HIGH, preferred_element_type=F32,
    )
    pl.semaphore_wait(barrier, len(partners) + seg)

    squares = PlaneSum(plane, own, column, line, n_sent, n_landed)

    def scales():
        scale = lax.rsqrt(squares.total(1) / (width * HEADS) + EPS)
        pick = (lax.broadcasted_iota(jnp.int32, (8, HD), 0) == 0).astype(F32)
        spread[...] = lax.dot_general(
            scale, pick, (((0,), (0,)), ((), ())), precision=HIGH, preferred_element_type=F32
        )

    piece = HD // SPAN
    whole = []
    size = rows // IN_UNITS

    def over(slot, unit, to):
        ref = kv.at[slot, pl.ds(unit * size, size)]
        return remote(ref, ref, kv_sent.at[1 + unit], kv_landed.at[1 + unit], to)

    def relay(slot, unit):
        ref = kv.at[slot, pl.ds(unit * size, size)]
        at = 1 + IN_UNITS + unit
        return remote(ref, ref, kv_sent.at[at], kv_landed.at[at], mate)


    def finish_rows(unit, total):
        at = unit.at
        rscale = spread[at]
        key = (total[:, HD : 2 * HD] * rscale).astype(BF16)
        value = (total[:, 2 * HD :] * rscale).astype(BF16)
        kv[pos, at, :HD] = key
        kv[pos, at, HD:] = value
        key = feat(key.astype(F32))
        product = lax.dot_general(key.astype(BF16), value, (((0,), (0,)), ((), ())), preferred_element_type=F32)
        amount = jnp.sum(key, axis=0, keepdims=True)
        whole[:] = [whole[0] + product, whole[1] + amount] if whole else [product, amount]
        q_ref[at] = (total[:, :HD] * rscale).astype(BF16)

    def begin():
        squares.start(0)
        loads[2].wait()
        for d in range(1, segments):
            @pl.when(seg - d >= 0)
            def _():
                pl.semaphore_signal(ready.at[d - 1], inc=1, device_id=later[segments - d - 1], device_id_type=MESH)

    units = make_units(plane, buf, g_sent, g_landed, rows, IN_UNITS, ())
    run_units(units, product_of(buf, w_ref, acc, finish_rows), [begin, squares.pass_on, scales])

    to_mate = remote(kv.at[pos], kv.at[pos], kv_sent.at[0], kv_landed.at[0], mate)
    from_mate = remote(kv.at[mate_slot], kv.at[mate_slot], kv_sent.at[0], kv_landed.at[0], mate)

    for at in range(SPAN):
        term[at, :piece] = whole[0][at * piece : (at + 1) * piece].astype(BF16)
        term[at, piece:] = jnp.broadcast_to(whole[1], (NORM_ROWS, HD)).astype(BF16)

    def first(step):
        return remote(term.at[lax.rem(pos + step, SPAN)], parts.at[step - 1],
                      a_sent.at[step - 1], a_landed.at[step - 1], peers[step])

    @pl.when(seg + 1 < segments)
    def _():
        for step in (2, 1, 3):
            first(step).start()

    @pl.when(pos < 2)
    def _():
        for unit in range(IN_UNITS // 2):
            over(pos, unit, across).start()

    to_mate.start()

    chunk = 128

    def attend(slot, causal):
        for r in range(rows // chunk):
            at = pl.ds(r * chunk, chunk)
            live = (r + 1) * chunk if causal else rows
            scores = lax.dot_general(
                q_ref[at], kv[slot, :live, :HD], (((1,), (1,)), ((), ())), preferred_element_type=F32
            )
            if causal:
                row = lax.broadcasted_iota(jnp.int32, (chunk, live), 0) + r * chunk
                scores = jnp.where(row >= lax.broadcasted_iota(jnp.int32, (chunk, live), 1), scores, -1e30)
            top = jnp.max(scores, axis=1, keepdims=True)
            if not causal:
                before = top_ref[at]
                top = jnp.maximum(top, before)
                shrink = jnp.exp2((before - top) * FACTOR)
            expo = jnp.exp2((scores - top) * FACTOR)
            weight = jnp.sum(expo, axis=1, keepdims=True)
            mixed = jnp.dot(expo.astype(BF16), kv[slot, :live, HD:], preferred_element_type=F32)
            if not causal:
                weight = weight + sum_ref[at] * shrink
                mixed = mixed + local_ref[at] * shrink
            top_ref[at] = top
            sum_ref[at] = weight
            local_ref[at] = mixed

    attend(pos, True)

    here = pl.ds(pl.multiple_of(pos * piece, 16), piece)

    @pl.when(seg + 1 < segments)
    def _():
        total = term[pos].astype(F32)
        for step in (1, 2, 3):
            first(step).wait_recv()
            total = total + parts[step - 1].astype(F32)
        outgoing[...] = total.astype(BF16)

    def second(d):
        return remote(outgoing, incoming.at[d - 1], b_sent.at[d - 1], b_landed.at[d - 1], later[d - 1])

    order = sorted(range(1, segments), key=lambda d: -min(d, segments - d))
    for d in order:
        @pl.when(seg + d < segments)
        def _():
            pl.semaphore_wait(ready.at[d - 1], 1)
            second(d).start()

    @pl.when(pos < 2)
    def _():
        for unit in range(IN_UNITS // 2, IN_UNITS):
            over(pos, unit, across).start()

    from_mate.wait_recv()

    @pl.when(mate_slot < pos)
    def _():
        attend(mate_slot, False)

    @pl.when(pos >= 2)
    def _():
        for unit in range(IN_UNITS):
            over(across_slot, unit, across).wait_recv()
            relay(across_slot, unit).start()

    queries = feat(q_ref[...].astype(F32)).astype(BF16)

    share[...] = jnp.zeros_like(share)
    for d in reversed(order):
        @pl.when(seg - d >= 0)
        def _():
            second(d).wait_recv()
            share[...] += incoming[d - 1].astype(F32)
    def third(step):
        return remote(memory.at[here], memory.at[here], c_sent.at[step - 1], c_landed.at[step - 1], peers[step])

    @pl.when(seg == 0)
    def _():
        memory[...] = jnp.zeros_like(memory)

    @pl.when(seg > 0)
    def _():
        memory[here] = share[:piece].astype(BF16)
        for step in (2, 1, 3):
            third(step).start()

    @pl.when(pos >= 2)
    def _():
        attend(across_slot, False)
        for unit in range(IN_UNITS):
            relay(relayed_slot, unit).wait_recv()
        attend(relayed_slot, False)

    gate = jax.nn.sigmoid(jnp.full((1, HD), gate_ref[0], F32))
    local_ref[...] = local_ref[...] * ((1.0 - gate) / sum_ref[...])

    pick = (lax.broadcasted_iota(jnp.int32, (8, HD), 0) == 0).astype(F32)
    norm = lax.dot_general(
        share[piece : piece + 8], pick, (((0,), (0,)), ((), ())), precision=HIGH, preferred_element_type=F32
    )
    denom = jnp.dot(queries, norm.astype(BF16), preferred_element_type=F32)
    weight = gate / jnp.maximum(denom, 1.0)

    @pl.when(seg > 0)
    def _():
        for step in (1, 2, 3):
            there = memory.at[pl.ds(pl.multiple_of(lax.rem(pos + SPAN - step, SPAN) * piece, 16), piece)]
            remote(there, there, c_sent.at[step - 1], c_landed.at[step - 1], peers[step]).wait_recv()

    numer = jnp.dot(queries, memory[...], preferred_element_type=F32)
    obuf[h] = (numer * weight + local_ref[...]).astype(BF16)

    loads[3].wait()
    out_units = make_units(plane, obuf, o_sent, o_landed, rows, OUT_UNITS, ("first",))

    def finish(unit, total):
        o_ref[unit.at] = total.astype(BF16)

    run_units(out_units, product_of(obuf, wo_ref, oacc, finish))

    for unit in units + out_units:
        unit.finish()
    squares.finish()
    to_mate.wait_send()

    @pl.when(seg + 1 < segments)
    def _():
        for step in (1, 2, 3):
            first(step).wait_send()

    @pl.when(seg > 0)
    def _():
        for step in (1, 2, 3):
            third(step).wait_send()

    @pl.when(pos < 2)
    def _():
        for unit in range(IN_UNITS):
            over(pos, unit, across).wait_send()

    @pl.when(pos >= 2)
    def _():
        for unit in range(IN_UNITS):
            relay(across_slot, unit).wait_send()

    for d in order:
        @pl.when(seg + d < segments)
        def _():
            second(d).wait_send()


def layer(gate, tokens, gain, weights, out_weights, segments):
    rows, width = tokens.shape
    columns, out_columns = weights.shape[2], out_weights.shape[2]
    piece = HD // SPAN
    anywhere = pl.BlockSpec(memory_space=pl.ANY)
    dma = pltpu.SemaphoreType.DMA
    return pl.pallas_call(
        functools.partial(layer_kernel, segments),
        out_shape=jax.ShapeDtypeStruct((rows, out_columns), BF16),
        in_specs=[pl.BlockSpec(memory_space=pltpu.SMEM)] + [anywhere] * 4,
        out_specs=pl.BlockSpec(memory_space=pltpu.VMEM),
        scratch_shapes=[
            pltpu.VMEM((rows, width), BF16),
            pltpu.VMEM((1, width), BF16),
            pltpu.VMEM((HEADS, width, columns), BF16),
            pltpu.VMEM((HEADS, HD, out_columns), BF16),
            pltpu.VMEM((HEADS, rows, width), BF16),
            pltpu.VMEM((rows, columns), F32),
            pltpu.VMEM((8, rows), F32),
            pltpu.VMEM((3, 8, rows), F32),
            pltpu.VMEM((4, 8, rows), F32),
            pltpu.VMEM((rows, HD), F32),
            pltpu.VMEM((rows, HD), BF16),
            pltpu.VMEM((SPAN, rows, 2 * HD), BF16),
            pltpu.VMEM((rows, 1), F32),
            pltpu.VMEM((rows, 1), F32),
            pltpu.VMEM((rows, HD), F32),
            pltpu.VMEM((SPAN, piece + NORM_ROWS, HD), BF16),
            pltpu.VMEM((3, piece + NORM_ROWS, HD), BF16),
            pltpu.VMEM((piece + NORM_ROWS, HD), BF16),
            pltpu.VMEM((segments - 1, piece + NORM_ROWS, HD), BF16),
            pltpu.VMEM((piece + NORM_ROWS, HD), F32),
            pltpu.VMEM((HD, HD), BF16),
            pltpu.VMEM((HEADS, rows, HD), BF16),
            pltpu.VMEM((rows, out_columns), F32),
            pltpu.SemaphoreType.REGULAR((segments - 1,)),
            dma((4,)),
            dma((IN_UNITS, 15)),
            dma((IN_UNITS, 15)),
            dma((6,)),
            dma((6,)),
            dma((1 + 2 * IN_UNITS,)),
            dma((1 + 2 * IN_UNITS,)),
            dma((3,)),
            dma((3,)),
            dma((segments - 1,)),
            dma((segments - 1,)),
            dma((3,)),
            dma((3,)),
            dma((OUT_UNITS, 15)),
            dma((OUT_UNITS, 15)),
        ],
        compiler_params=pltpu.CompilerParams(collective_id=0, has_side_effects=True, vmem_limit_bytes=56 << 20),
        name="layer",
    )(gate, tokens, gain, weights, out_weights)


def on_device(tokens, norm_gain, qkv_weight, out_weight, mem_gate):
    weights = qkv_weight.reshape(HEADS, tokens.shape[1], 3 * HD)
    out_weights = out_weight.reshape(HEADS, HD, out_weight.shape[1])
    return layer(mem_gate, tokens, norm_gain, weights, out_weights, lax.axis_size("seq") // SPAN)


def solution(mesh):
    placed = (P("seq", "head"), P(None, "head"), P(None, "head", None), P(None, "head"), P("head"))
    return jax.shard_map(
        on_device, mesh=mesh, in_specs=placed, out_specs=P("seq", "head"), check_vma=False
    )
```
